256 devices in a mesh: row: 8 (over x_lo, y), col: 32 (over z, x_hi, core).
Axes of the slice: x: 4 (x_hi: 2, x_lo: 2; x = x_hi * 2 + x_lo), y: 4, z: 8, core: 2. Of those that a mesh axis runs over, the one named last changes fastest.
Arguments:
- tile_values: bfloat16 [8, 32, 32, 3, 128, 128], P('row', 'col'), may hold values from -6 to 6
- tile_slots: int32 [8, 32, 32, 3, 3], P('row', 'col'), may hold values from 0 to 59, as said below
- counts: int32 [8, 32, 32], P('row', 'col'), may hold values from 1 to 3, as said below
- factor: bfloat16 [32768, 128], P(('row', 'col'))
- d_factor: bfloat16 [32768, 128], P(('row', 'col'))
- core_rel: bfloat16 [60, 128, 128], replicated, may hold values from -0.5 to 0.5
- d_core: bfloat16 [60, 128, 128], replicated, may hold values from -0.5 to 0.5
Outputs:
- hv_factor: bfloat16 [32768, 128], P(('row', 'col'))
- hv_core: float32 [60, 128, 128], replicated
The draws below stay inside these ranges and needn't reach their ends.
Inputs may be any that keep to these rules, and one draw needn't show every extreme that they name: `counts`: every device has, for every row span, at least one live slot, and in every draw some row span of every device has exactly 3 live slots. `tile_slots`: the three entries of a slot are a relation below 60, a row tile that is always 0 (each row span is one tile) and a column tile below 8; dead slots hold such entries too.
All inputs are finite; a program needn't handle non-finite values.
Results may differ from the reference program's by a relative error of at most 0.002.
The reference program's roundings to bfloat16 on the way count: a program that leaves them out, or rounds other values in their place, can miss the bound.
Values may be sent and summed in bfloat16 or wider, within the bound.
No kernel may reach another device: no remote copies, remote signals or barrier semaphores. Data moves between devices by JAX's collectives and lax.ppermute only.
A program may use at most 128 MiB of HBM per device.

```python
import math
import jax
import jax.numpy as jnp
from jax import lax

TILE = 128
RANK = 128
RELS = 60
E_DEV = 128
SC = 3
ENT = 32768
N_ROW = 8
N_COL = 32


def entity_scale(key, level):
    position = jnp.arange(ENT, dtype=jnp.float32) / ENT
    jitter = jax.random.uniform(jax.random.fold_in(key, 11), (ENT, 1), minval=0.0, maxval=math.log(3.0))
    return level * jnp.exp(math.log(3.0) * position[:, None] + jitter)


def entity_rows(key, level):
    scale = entity_scale(key, level)
    values = jax.random.normal(jax.random.fold_in(key, 5), (ENT, RANK)) * scale
    return values.astype(jnp.bfloat16)


def draw_factor(key, part):
    key = jax.random.fold_in(key, 1)
    return entity_rows(key, 0.003)


def draw_d_factor(key, part):
    key = jax.random.fold_in(key, 2)
    return entity_rows(key, 0.003)


def draw_tile_slots(key, part):
    key = jax.random.fold_in(key, 3)
    shape = (N_ROW, N_COL, N_COL, SC)
    relation = jax.random.randint(jax.random.fold_in(key, 1), shape, 0, RELS)
    row_tile = jax.random.randint(jax.random.fold_in(key, 2), shape, 0, E_DEV // TILE)
    col_tile = jax.random.randint(jax.random.fold_in(key, 3), shape, 0, N_ROW * E_DEV // TILE)
    relation = relation.at[0, 0, 0, 0].set(RELS - 1)
    col_tile = col_tile.at[0, 0, 0, 0].set(N_ROW * E_DEV // TILE - 1)
    return jnp.stack([relation, row_tile, col_tile], axis=-1).astype(jnp.int32)


def draw_counts(key, part):
    key = jax.random.fold_in(key, 4)
    drawn = jax.random.randint(jax.random.fold_in(key, 1), (N_ROW, N_COL, N_COL), 1, SC + 1)
    chosen = jax.random.randint(jax.random.fold_in(key, 2), (N_ROW, N_COL, 1), 0, N_COL)
    groups = jnp.arange(N_COL, dtype=jnp.int32)[None, None, :]
    return jnp.where(groups == chosen, SC, drawn).astype(jnp.int32)


def block_scale(rng, dims, cuts, smallest, top_value):
    def one(dim, parts):
        draws = jax.random.uniform(jax.random.fold_in(jax.random.fold_in(rng, 6), dim), (parts,), jnp.float32, smallest / len(cuts), top_value / len(cuts))
        return jnp.repeat(jnp.exp(draws), dims[dim] // parts).reshape((-1,) + (1,) * (len(dims) - dim - 1))

    factor_of = one(*cuts[0])
    for cut in cuts[1:]:
        factor_of = factor_of * one(*cut)
    return factor_of


def normal_values(stream_key, dims, scale, reach, split=(), kind=jnp.bfloat16):
    array = scale * jax.random.normal(stream_key, dims, jnp.float32)
    if split:
        array = array * block_scale(stream_key, dims, split, -0.22, 0.18)
    return jnp.clip(array, -reach, reach).astype(kind)


def setup_inputs(seed: int = 0) -> dict:
    splits = jax.random.split(jax.random.key(seed), 8)
    tile_values = normal_values(splits[0], (N_ROW, N_COL, N_COL, SC, TILE, TILE), 1.0, 6.0, ((0, 8), (1, 32)))
    tile_slots = draw_tile_slots(jax.random.fold_in(splits[7], 71), 0)
    counts = draw_counts(jax.random.fold_in(splits[7], 71), 0)
    factor = draw_factor(jax.random.fold_in(splits[7], 71), 0)
    d_factor = draw_d_factor(jax.random.fold_in(splits[7], 71), 0)
    core_rel = normal_values(splits[5], (RELS, RANK, RANK), RANK ** -0.5, 0.5)
    d_core = normal_values(splits[6], (RELS, RANK, RANK), RANK ** -0.5, 0.5)
    return {"tile_values": tile_values, "tile_slots": tile_slots, "counts": counts, "factor": factor, "d_factor": d_factor, "core_rel": core_rel, "d_core": d_core}


HIGH = lax.Precision.HIGHEST


def core_direction(gram, d_gram, core_rel, d_core, core_sum):
    relation = core_rel.astype(jnp.float32)
    d_relation = d_core.astype(jnp.float32)
    left = jnp.einsum('ab,kbc->kac', d_gram, relation, precision=HIGH) + jnp.einsum('ab,kbc->kac', gram, d_relation, precision=HIGH)
    right = jnp.einsum('ab,kbc->kac', gram, relation, precision=HIGH)
    result = jnp.einsum('kac,cd->kad', left, gram, precision=HIGH) + jnp.einsum('kac,cd->kad', right, d_gram, precision=HIGH)
    return result - core_sum


def rounded(values):
    return lax.optimization_barrier(values.astype(jnp.bfloat16)).astype(jnp.float32)


def reference(tile_values, tile_slots, counts, factor, d_factor, core_rel, d_core):
    pair = jnp.concatenate([d_factor, factor], axis=1)
    slot_count = N_COL * SC
    group_ids = jnp.repeat(jnp.arange(N_COL, dtype=jnp.int32), SC)
    offsets = jnp.arange(TILE, dtype=jnp.int32)
    take_rows = jax.vmap(lambda begin: lax.dynamic_slice_in_dim(pair, begin, TILE, 0))

    def device_step(carry, device):
        total, core_sum = carry
        row_id = device // N_COL
        col_id = device % N_COL
        block = tile_values[row_id, col_id].reshape(slot_count, TILE, TILE)
        index = tile_slots[row_id, col_id].reshape(slot_count, 3)
        live = (jnp.arange(SC, dtype=jnp.int32)[None, :] < counts[row_id, col_id][:, None]).reshape(slot_count)
        block = jnp.where(live[:, None, None], block, jnp.zeros_like(block)).astype(jnp.float32)
        row_start = ((row_id * N_COL + group_ids) * E_DEV + index[:, 1] * TILE).astype(jnp.int32)
        col_pos = index[:, 2] * TILE
        col_start = (((col_pos // E_DEV) * N_COL + col_id) * E_DEV + col_pos % E_DEV).astype(jnp.int32)
        rows_fac = take_rows(row_start).astype(jnp.float32)
        cols_fac = take_rows(col_start).astype(jnp.float32)
        near = rounded(jnp.einsum('suv,svc->suc', block, cols_fac, precision=HIGH))
        far = rounded(jnp.einsum('suv,suc->svc', block, rows_fac, precision=HIGH))
        relation = jnp.take(core_rel, index[:, 0], axis=0).astype(jnp.float32)
        d_relation = jnp.take(d_core, index[:, 0], axis=0).astype(jnp.float32)
        row_term = jnp.einsum('suq,srq->sur', near[..., :RANK], relation, precision=HIGH) + jnp.einsum('suq,srq->sur', near[..., RANK:], d_relation, precision=HIGH)
        col_term = jnp.einsum('svq,sqr->svr', far[..., :RANK], relation, precision=HIGH) + jnp.einsum('svq,sqr->svr', far[..., RANK:], d_relation, precision=HIGH)
        core_slot = jnp.einsum('sua,sub->sab', rows_fac[..., RANK:], near[..., :RANK], precision=HIGH) + jnp.einsum('sua,sub->sab', rows_fac[..., :RANK], near[..., RANK:], precision=HIGH)
        total = total.at[row_start[:, None] + offsets[None, :]].add(row_term)
        total = total.at[col_start[:, None] + offsets[None, :]].add(col_term)
        core_sum = core_sum.at[index[:, 0]].add(core_slot)
        return (total, core_sum), None

    start_carry = (jnp.zeros((ENT, RANK), jnp.float32), jnp.zeros((RELS, RANK, RANK), jnp.float32))
    (total, core_sum), _ = lax.scan(device_step, start_carry, jnp.arange(N_ROW * N_COL, dtype=jnp.int32))
    hv_factor = (-total).astype(jnp.bfloat16)
    gram = jnp.dot(factor.T, factor, preferred_element_type=jnp.float32)
    cross = jnp.dot(factor.T, d_factor, preferred_element_type=jnp.float32)
    d_gram = cross + cross.T
    hv_core = core_direction(gram, d_gram, core_rel, d_core, core_sum)
    return hv_factor, hv_core
```

```python
import jax
import jax.numpy as jnp
from jax import lax
from jax.experimental import pallas as pl
from jax.experimental.pallas import tpu as pltpu
from jax.sharding import Mesh
from jax.sharding import PartitionSpec as P

F32 = jnp.float32
BF16 = jnp.bfloat16
I16 = jnp.int16
I32 = jnp.int32
HIGH = lax.Precision.HIGHEST

T = 128
SC = 3
NR = 8
NQ = 16
RELS = 60
HALF = RELS // 2 * T
PART = HALF // NR
PIECE = 32
GRP = 160
NGRP = HALF // GRP
SEND_CORE = NQ * T
SEND_EXP = SEND_CORE + HALF
SEND_ROWS = SEND_EXP + 48
C1_CORE = T
C1_GRAM = C1_CORE + PART
C1_EXP = C1_GRAM + 32
C1_ROWS = C1_EXP + 16
C2_CORE = T
C2_GRAM = C2_CORE + PIECE
C2_EXP = C2_GRAM + 32
C2_ROWS = C2_EXP + 16
P3_ROWS = PIECE + 16
P4_ROWS = PART + 16

NT = (((1,), (1,)), ((), ()))
TN = (((0,), (0,)), ((), ()))


def exponent_of(x):
    top = jnp.max(jnp.abs(x), axis=0, keepdims=True)
    e = jnp.floor(jnp.log2(jnp.maximum(top, 1e-37))) + 1.0
    return jnp.clip(e, -100.0, 127.0)


def coded(x, e):
    q = jnp.round(x * jnp.exp2(15.0 - e))
    return jnp.clip(q, -32767.0, 32767.0).astype(I32)


def enc(x):
    e = exponent_of(x)
    return coded(x, e).astype(I16), e


def enc_wide(x):
    e = exponent_of(x)
    q = x * jnp.exp2(15.0 - e)
    hi = jnp.clip(jnp.round(q), -32767.0, 32767.0)
    lo = jnp.clip(jnp.round((q - hi) * 16384.0), -32767.0, 32767.0)
    return hi.astype(I32).astype(I16), lo.astype(I32).astype(I16), e


def dec(q, e):
    return q.astype(I32).astype(F32) * jnp.exp2(e - 15.0)


def dec_wide(hi, lo, e):
    return (hi.astype(I32).astype(F32) + lo.astype(I32).astype(F32) * (1.0 / 16384.0)) * jnp.exp2(e - 15.0)


def exps_of(block):
    return block.astype(I32).astype(F32)


def exps_block(rows):
    place = lax.broadcasted_iota(I32, (16, T), 0)
    out = jnp.zeros((16, T), F32)
    for r, e in enumerate(rows):
        out = jnp.where(place == r, e, out)
    return out.astype(I32).astype(I16)


def main_kernel(slots, counts, meta, x_ref, mine_ref, other_ref, col_ref, r_ref, dr_ref,
                send_ref, keep_row_ref, keep_core_ref, colt_ref, gram_ref,
                core_acc, gram_acc, rows_s, exps):
    h = pl.program_id(0)
    q = pl.program_id(1)
    c = meta[0]
    span = q * 2 + jnp.where(h == 0, c, 1 - c)

    @pl.when((h == 0) & (q == 0))
    def _():
        core_acc[...] = jnp.zeros_like(core_acc)
        gram_acc[...] = jnp.zeros_like(gram_acc)
        colt_ref[...] = jnp.zeros_like(colt_ref)
        exps[...] = jnp.zeros_like(exps)

    @pl.when(h == 0)
    def _():
        rows_s[...] = mine_ref[0]

    @pl.when(h == 1)
    def _():
        rows_s[...] = other_ref[0]

    rows = rows_s[...]
    rows_t = rows.T
    lhs_core = jnp.concatenate([rows_t[T:], rows_t[:T]], axis=1)
    gram_acc[...] += jnp.dot(rows_t[T:], rows, preferred_element_type=F32)
    total = None
    for s in range(SC):
        live = s < counts[span]
        base = (span * SC + s) * 3
        k = slots[base]
        b = slots[base + 2]
        x = x_ref[0, 0, 0, s]
        x = jnp.where(live, x, jnp.zeros_like(x))
        near = jnp.dot(x, col_ref[b], preferred_element_type=F32).astype(BF16)
        far = lax.dot_general(x, rows, TN, preferred_element_type=F32).astype(BF16)
        r = r_ref[k]
        dr = dr_ref[k]
        row_term = lax.dot_general(near, jnp.concatenate([r, dr], axis=1), NT, preferred_element_type=F32)
        total = row_term if total is None else total + row_term
        colt_ref[b] += jnp.dot(far, jnp.concatenate([r, dr], axis=0), preferred_element_type=F32)
        place = pl.ds(pl.multiple_of(k * T, T), T)
        core_acc[place] += jnp.dot(lhs_core, jnp.concatenate([near[:, :T], near[:, T:]], axis=0),
                                   preferred_element_type=F32)

    @pl.when(h == 0)
    def _():
        keep_row_ref[q] = total

    @pl.when(h == 1)
    def _():
        val, e = enc(total)
        send_ref[pl.ds(pl.multiple_of(q * T, T), T)] = val
        exps[pl.ds(q, 1)] = e

    @pl.when((h == 1) & (q == NQ - 1))
    def _():
        keep_core_ref[...] = core_acc[pl.ds(pl.multiple_of(c * HALF, HALF), HALF)]
        start = (1 - c) * HALF

        def body(g, carry):
            val, e = enc(core_acc[pl.ds(pl.multiple_of(start + g * GRP, 32), GRP)])
            send_ref[pl.ds(pl.multiple_of(SEND_CORE + g * GRP, 32), GRP)] = val
            exps[pl.ds(NQ + g, 1)] = e
            return carry

        lax.fori_loop(0, NGRP, body, 0)
        send_ref[SEND_EXP:] = exps[...].astype(I32).astype(I16)
        part = gram_acc[pl.ds(pl.multiple_of(meta[1] * 8, 8), 8)]
        gram_ref[0:8] = part[:, :T]
        gram_ref[8:16] = part[:, T:]


def merge_kernel(recv_ref, keep_core_ref, colt_ref, gram_ref, out_ref):
    exps = exps_of(recv_ref[SEND_EXP:])
    g_hi, g_lo, g_e = enc_wide(gram_ref[...])
    for i in range(NR):
        val, e0 = enc(colt_ref[i])
        out_ref[i, 0:T] = val
        rows = [e0]
        for j in range(PART // GRP):
            g = i * (PART // GRP) + j
            got = dec(recv_ref[SEND_CORE + g * GRP:SEND_CORE + (g + 1) * GRP], exps[NQ + g:NQ + g + 1])
            val, e = enc(got + keep_core_ref[g * GRP:(g + 1) * GRP])
            out_ref[i, C1_CORE + j * GRP:C1_CORE + (j + 1) * GRP] = val
            rows.append(e)
        out_ref[i, C1_GRAM:C1_GRAM + 16] = g_hi
        out_ref[i, C1_GRAM + 16:C1_GRAM + 32] = g_lo
        rows.append(g_e)
        out_ref[i, C1_EXP:C1_ROWS] = exps_block(rows)


def second_kernel(r1_ref, recv_ref, keep_row_ref, out_ref, cols_ref, core_s):
    col = jnp.zeros((T, T), F32)
    gram = jnp.zeros((16, T), F32)
    core = [jnp.zeros((GRP, T), F32) for _ in range(PART // GRP)]
    all_e = [exps_of(r1_ref[i, C1_EXP:C1_ROWS]) for i in range(NR)]
    for i in range(NR):
        e = all_e[i]
        col = col + dec(r1_ref[i, 0:T], e[0:1])
        gram = gram + dec_wide(r1_ref[i, C1_GRAM:C1_GRAM + 16], r1_ref[i, C1_GRAM + 16:C1_GRAM + 32], e[4:5])
    cols_ref[...] = col
    for j in range(PART // GRP):
        acc = jnp.zeros((GRP, T), F32)
        for i in range(NR):
            acc = acc + dec(r1_ref[i, C1_CORE + j * GRP:C1_CORE + (j + 1) * GRP], all_e[i][1 + j:2 + j])
        core_s[j * GRP:(j + 1) * GRP] = acc
    core_s[PART:] = jnp.zeros((PIECE, T), F32)
    exps = exps_of(recv_ref[SEND_EXP:])
    g_hi, g_lo, g_e = enc_wide(gram)
    for q in range(NQ):
        got = dec(recv_ref[q * T:(q + 1) * T], exps[q:q + 1])
        val, e0 = enc(got + keep_row_ref[q])
        out_ref[q, 0:T] = val
        val, e1 = enc(core_s[q * PIECE:(q + 1) * PIECE])
        out_ref[q, C2_CORE:C2_CORE + PIECE] = val
        out_ref[q, C2_GRAM:C2_GRAM + 16] = g_hi
        out_ref[q, C2_GRAM + 16:C2_GRAM + 32] = g_lo
        out_ref[q, C2_EXP:C2_ROWS] = exps_block([e0, e1, g_e])


def third_kernel(meta, r2_ref, cols_ref, r_ref, dr_ref, hv_ref, out_ref, gram_s, cross_s):
    total = cols_ref[...]
    core = jnp.zeros((PIECE, T), F32)
    for q in range(NQ):
        e = exps_of(r2_ref[q, C2_EXP:C2_ROWS])
        total = total + dec(r2_ref[q, 0:T], e[0:1])
        core = core + dec(r2_ref[q, C2_CORE:C2_CORE + PIECE], e[1:2])
        g = dec_wide(r2_ref[q, C2_GRAM:C2_GRAM + 16], r2_ref[q, C2_GRAM + 16:C2_GRAM + 32], e[2:3])
        cross_s[q * 8:(q + 1) * 8] = g[0:8]
        gram_s[q * 8:(q + 1) * 8] = g[8:16]
    hv_ref[...] = (-total).astype(BF16)
    gram = gram_s[...]
    cross = cross_s[...]
    cross_s[...] = cross + cross.T
    d_gram = cross_s[...]
    r = r_ref[0].astype(F32)
    dr = dr_ref[0].astype(F32)
    rows = pl.ds(pl.multiple_of(meta[3], PIECE), PIECE)
    g_rows = gram_s[rows]
    d_rows = cross_s[rows]
    mm = lambda a, b: jnp.dot(a, b, precision=HIGH, preferred_element_type=F32)
    left = mm(d_rows, r) + mm(g_rows, dr)
    right = mm(g_rows, r)
    piece = mm(left, gram) + mm(right, d_gram) - core
    val, e = enc(piece)
    block = exps_block([e])
    for q in range(NQ):
        out_ref[q, 0:PIECE] = val
        out_ref[q, PIECE:P3_ROWS] = block


def fourth_kernel(r3_ref, out_ref):
    place = lax.broadcasted_iota(I32, (16, T), 0)
    exps = jnp.zeros((16, T), F32)
    for q in range(NQ - 1):
        exps = jnp.where(place == q, exps_of(r3_ref[q, PIECE:P3_ROWS])[0:1], exps)
    exps = exps.astype(I32).astype(I16)
    for i in range(NR):
        for q in range(NQ - 1):
            out_ref[i, q * PIECE:(q + 1) * PIECE] = r3_ref[q, 0:PIECE]
        out_ref[i, PART:P4_ROWS] = exps


def last_kernel(meta, mine_ref, other_ref, out_ref):
    h = pl.program_id(0)

    def put(ref):
        e = exps_of(ref[0, PART:P4_ROWS])
        for q in range(NQ - 1):
            out_ref[q * PIECE:(q + 1) * PIECE] = dec(ref[0, q * PIECE:(q + 1) * PIECE], e[q:q + 1])

    @pl.when(h == 0)
    def _():
        put(mine_ref)

    @pl.when(h == 1)
    def _():
        put(other_ref)


def shape(*dims, dtype=F32):
    return jax.ShapeDtypeStruct(dims, dtype)


WHOLE = pl.BlockSpec(memory_space=pltpu.VMEM)
BIG = pltpu.CompilerParams(vmem_limit_bytes=48 * 1024 * 1024)


def per_device(tile_values, tile_slots, counts, factor, d_factor, core_rel, d_core):
    swap = lambda a: lax.ppermute(a, "core", [(0, 1), (1, 0)])
    zx = lax.axis_index("z") * 2 + lax.axis_index("xh")
    row = lax.axis_index("xl") * 4 + lax.axis_index("y")
    core = lax.axis_index("core")
    first = core * HALF + row * PART + zx * PIECE
    meta = jnp.stack([core, zx, jnp.minimum(first // T, RELS - 1), first % T]).astype(I32)

    pair = jnp.concatenate([d_factor, factor], axis=1)
    mine = lax.all_to_all(jnp.broadcast_to(pair[None], (NQ, T, 2 * T)), ("z", "xh"), 0, 0, tiled=True)
    other = swap(mine)
    columns = lax.all_to_all(jnp.broadcast_to(pair[None], (NR, T, 2 * T)), ("xl", "y"), 0, 0, tiled=True)

    span_of = lambda h, q, m: q * 2 + jnp.where(h == 0, m[0], 1 - m[0])
    send, keep_row, keep_core, colt, gram = pl.pallas_call(
        main_kernel,
        grid_spec=pltpu.PrefetchScalarGridSpec(
            num_scalar_prefetch=3,
            grid=(2, NQ),
            in_specs=[
                pl.BlockSpec((1, 1, 1, SC, T, T), lambda h, q, s, n, m: (0, 0, span_of(h, q, m), 0, 0, 0)),
                pl.BlockSpec((1, T, 2 * T), lambda h, q, s, n, m: (jnp.where(h == 0, q, NQ - 1), 0, 0)),
                pl.BlockSpec((1, T, 2 * T), lambda h, q, s, n, m: (jnp.where(h == 0, 0, q), 0, 0)),
                WHOLE, WHOLE, WHOLE,
            ],
            out_specs=[WHOLE] * 5,
            scratch_shapes=[
                pltpu.VMEM((RELS * T, T), F32),
                pltpu.VMEM((T, 2 * T), F32),
                pltpu.VMEM((T, 2 * T), BF16),
                pltpu.VMEM((48, T), F32),
            ],
        ),
        out_shape=[shape(SEND_ROWS, T, dtype=I16), shape(NQ, T, T), shape(HALF, T), shape(NR, T, T), shape(16, T)],
        compiler_params=BIG,
    )(tile_slots.reshape(-1), counts.reshape(-1), meta, tile_values, mine, other, columns, core_rel, d_core)

    recv = swap(send)
    c1 = pl.pallas_call(
        merge_kernel,
        in_specs=[WHOLE] * 4, out_specs=WHOLE,
        out_shape=shape(NR, C1_ROWS, T, dtype=I16), compiler_params=BIG,
    )(recv, keep_core, colt, gram)
    r1 = lax.all_to_all(c1, ("xl", "y"), 0, 0, tiled=True)
    c2, cols = pl.pallas_call(
        second_kernel,
        in_specs=[WHOLE] * 3, out_specs=[WHOLE] * 2,
        out_shape=[shape(NQ, C2_ROWS, T, dtype=I16), shape(T, T)],
        scratch_shapes=[pltpu.VMEM((PART + PIECE, T), F32)], compiler_params=BIG,
    )(r1, recv, keep_row)
    r2 = lax.all_to_all(c2, ("z", "xh"), 0, 0, tiled=True)
    hv_factor, c3 = pl.pallas_call(
        third_kernel,
        grid_spec=pltpu.PrefetchScalarGridSpec(
            num_scalar_prefetch=1,
            grid=(1,),
            in_specs=[
                WHOLE, WHOLE,
                pl.BlockSpec((1, T, T), lambda i, m: (m[2], 0, 0)),
                pl.BlockSpec((1, T, T), lambda i, m: (m[2], 0, 0)),
            ],
            out_specs=[WHOLE, WHOLE],
            scratch_shapes=[pltpu.VMEM((T, T), F32), pltpu.VMEM((T, T), F32)],
        ),
        out_shape=[shape(T, T, dtype=BF16), shape(NQ, P3_ROWS, T, dtype=I16)],
        compiler_params=BIG,
    )(meta, r2, cols, core_rel, d_core)
    r3 = lax.all_to_all(c3, ("z", "xh"), 0, 0, tiled=True)
    c4 = pl.pallas_call(
        fourth_kernel,
        in_specs=[WHOLE], out_specs=WHOLE,
        out_shape=shape(NR, P4_ROWS, T, dtype=I16), compiler_params=BIG,
    )(r3)
    r4 = lax.all_to_all(c4, ("xl", "y"), 0, 0, tiled=True)
    r5 = swap(r4)
    hv_core = pl.pallas_call(
        last_kernel,
        grid_spec=pltpu.PrefetchScalarGridSpec(
            num_scalar_prefetch=1,
            grid=(2, NR),
            in_specs=[
                pl.BlockSpec((1, P4_ROWS, T), lambda h, i, m: (jnp.where(h == 0, i, NR - 1), 0, 0)),
                pl.BlockSpec((1, P4_ROWS, T), lambda h, i, m: (jnp.where(h == 0, 0, i), 0, 0)),
            ],
            out_specs=pl.BlockSpec((PART, T), lambda h, i, m: (jnp.where(h == 0, m[0], 1 - m[0]) * NR + i, 0)),
        ),
        out_shape=shape(RELS * T, T), compiler_params=BIG,
    )(meta, r4, r5)
    return hv_factor, hv_core.reshape(RELS, T, T)


def solution(mesh):
    chips = Mesh(mesh.devices.reshape(2, 4, 8, 2, 2), ("xl", "y", "z", "xh", "core"))
    row, col = ("xl", "y"), ("z", "xh", "core")
    placed = (
        P(row, col, None, None, None, None),
        P(row, col, None, None, None),
        P(row, col, None),
        P(row + col, None),
        P(row + col, None),
        P(),
        P(),
    )
    return jax.shard_map(
        per_device,
        mesh=chips,
        in_specs=placed,
        out_specs=(P(row + col, None), P()),
        check_vma=False,
    )
```

```python
import jax
import jax.numpy as jnp
from jax import lax
from jax.experimental import pallas as pl
from jax.experimental.pallas import tpu as pltpu
from jax.sharding import Mesh
from jax.sharding import PartitionSpec as P

F32 = jnp.float32
BF16 = jnp.bfloat16
I16 = jnp.int16
I32 = jnp.int32
HIGH = lax.Precision.HIGHEST

T = 128
SC = 3
SPANS = 32
NR = 8
NZ = 8
UNROLL = 8
STEPS = SPANS // UNROLL
NG = 16
NQ = 16
RELS = 60
HALF = RELS // 2 * T
PIECE = HALF // NG
ROW_EXP = NQ * T
CORE_EXP = HALF
XH_EXP = NZ * T
C1_CORE = T // 2
C1_GRAM = C1_CORE + PIECE
C1_EXP = C1_GRAM + 32
C1_ROWS = C1_EXP + 16
C2_CORE = T
C2_GRAM = C2_CORE + PIECE
C2_EXP = C2_GRAM + 32
C2_ROWS = C2_EXP + 16
C3_ROWS = PIECE + 16

NT = (((1,), (1,)), ((), ()))
TN = (((0,), (0,)), ((), ()))


def exponent_of(x):
    top = jnp.max(jnp.abs(x), axis=0, keepdims=True)
    e = jnp.floor(jnp.log2(jnp.maximum(top, 1e-37))) + 1.0
    return jnp.clip(e, -100.0, 127.0)


def coded(x, e):
    q = jnp.round(x * jnp.exp2(15.0 - e))
    return jnp.clip(q, -32767.0, 32767.0).astype(I32)


def enc(x):
    e = exponent_of(x)
    return coded(x, e).astype(I16), e


def enc_wide(x):
    e = exponent_of(x)
    q = x * jnp.exp2(15.0 - e)
    hi = jnp.clip(jnp.round(q), -32767.0, 32767.0)
    lo = jnp.clip(jnp.round((q - hi) * 16384.0), -32767.0, 32767.0)
    return hi.astype(I32).astype(I16), lo.astype(I32).astype(I16), e


def dec(q, e):
    return q.astype(I32).astype(F32) * jnp.exp2(e - 15.0)


def dec_wide(hi, lo, e):
    return (hi.astype(I32).astype(F32) + lo.astype(I32).astype(F32) * (1.0 / 16384.0)) * jnp.exp2(e - 15.0)


def exps_of(block):
    return block.astype(I32).astype(F32)


def exps_block(rows):
    place = lax.broadcasted_iota(I32, (16, T), 0)
    out = jnp.zeros((16, T), F32)
    for r, e in enumerate(rows):
        out = jnp.where(place == r, e, out)
    return out.astype(I32).astype(I16)


def pair_kernel(d_hbm, f_hbm, wide_ref, one_ref, d_s, f_s, sems):
    one = pltpu.make_async_copy(d_hbm, d_s, sems.at[0])
    two = pltpu.make_async_copy(f_hbm, f_s, sems.at[1])
    one.start()
    two.start()
    one.wait()
    two.wait()
    one_ref[:, 0:T] = d_s[...]
    one_ref[:, T:] = f_s[...]
    for i in range(NZ):
        wide_ref[i] = one_ref[...]


def near_kernel(slots, counts, meta, x_hbm, r_hbm, dr_hbm, c0, c1, c2, c3,
                near_ref, total_ref, send_ref, x_s, r_s, dr_s, col_s, exps, sems):
    tiles = [pltpu.make_async_copy(x_hbm.at[pl.ds(n * UNROLL, UNROLL)], x_s.at[pl.ds(n * UNROLL, UNROLL)], sems.at[n])
             for n in range(STEPS)]
    cores = [pltpu.make_async_copy(r_hbm, r_s, sems.at[STEPS]), pltpu.make_async_copy(dr_hbm, dr_s, sems.at[STEPS + 1])]
    for copy in tiles + cores:
        copy.start()
    for n, ref in enumerate((c0, c1, c2, c3)):
        col_s[2 * n] = ref[0]
        col_s[2 * n + 1] = ref[1]
    xl, y = meta[5], meta[6]

    for step in range(STEPS):
        tiles[step].wait()
        for j in range(UNROLL):
            span = step * UNROLL + j
            for s in range(SC):
                b = slots[s, 2, span]
                at = ((y - b) & 3) * 2 + ((b >> 2) ^ xl)
                x = x_s[span, s]
                x = jnp.where(s < counts[span], x, jnp.zeros_like(x))
                near_ref[span, s] = jnp.dot(x, col_s[at], preferred_element_type=F32).astype(BF16)
    for copy in cores:
        copy.wait()

    def body(step, carry):
        for j in range(UNROLL):
            span = step * UNROLL + j
            total = None
            for s in range(SC):
                k = slots[s, 0, span]
                both = jnp.concatenate([r_s[k], dr_s[k]], axis=1)
                term = lax.dot_general(near_ref[span, s], both, NT, preferred_element_type=F32)
                total = term if total is None else total + term
            total_ref[span] = total
        return carry

    lax.fori_loop(0, STEPS, body, 0)

    def code(q, carry):
        val, e = enc(total_ref[q * 2 + 1 - meta[0]])
        send_ref[pl.ds(pl.multiple_of(q * T, T), T)] = val
        exps[pl.ds(q, 1)] = e
        return carry

    lax.fori_loop(0, NQ, code, 0, unroll=4)
    send_ref[ROW_EXP:] = exps[...].astype(I32).astype(I16)


def spans_of(meta, z, far_chip):
    c = meta[0]
    xh = 1 - meta[2] if far_chip else meta[2]
    return z * 4 + xh * 2 + c, z * 4 + xh * 2 + 1 - c


def core_sums(far_chip, slots, meta, refs, near_ref, core_ref, gram_ref):
    core_ref[...] = jnp.zeros_like(core_ref)
    gram_ref[...] = jnp.zeros_like(gram_ref)

    def body(step, carry):
        gram = jnp.zeros((T, 2 * T), F32)
        for j in range(UNROLL // 2):
            z = step * (UNROLL // 2) + j
            for span, ref in zip(spans_of(meta, z, far_chip), refs):
                rows = ref[z]
                rows_t = rows.T
                gram = gram + jnp.dot(rows_t[T:], rows, preferred_element_type=F32)
                lhs = jnp.concatenate([rows_t[T:], rows_t[:T]], axis=1)
                for s in range(SC):
                    k = slots[s, 0, span]
                    near = near_ref[span, s]
                    place = pl.ds(pl.multiple_of(k * T, T), T)
                    core_ref[place] += jnp.dot(lhs, jnp.concatenate([near[:, :T], near[:, T:]], axis=0),
                                               preferred_element_type=F32)
        gram_ref[...] += gram
        return carry

    lax.fori_loop(0, NZ * 2 // UNROLL, body, 0)


def core_kernel_a(slots, meta, r0, r1, near_ref, core_ref, gram_ref):
    core_sums(False, slots, meta, (r0, r1), near_ref, core_ref, gram_ref)


def core_kernel_b(slots, meta, r0, r1, near_ref, held_ref, gram_held, after, core_ref, send_ref, gram_out, gram_acc, exps):
    core_sums(True, slots, meta, (r0, r1), near_ref, core_ref, gram_acc)
    start = (1 - meta[0]) * HALF

    def code(g, carry):
        at = pl.ds(pl.multiple_of(start + g * PIECE, 16), PIECE)
        val, e = enc(core_ref[at] + held_ref[at])
        send_ref[pl.ds(pl.multiple_of(g * PIECE, 16), PIECE)] = val
        exps[pl.ds(g, 1)] = e
        return carry

    lax.fori_loop(0, NG, code, 0, unroll=4)
    send_ref[CORE_EXP:] = exps[...].astype(I32).astype(I16)
    at = pl.ds(pl.multiple_of(meta[1] * 8, 8), 8)
    part = gram_acc[at] + gram_held[at]
    gram_out[0:8] = part[:, :T]
    gram_out[8:16] = part[:, T:]


def far_sums(far_chip, slots, counts, meta, refs, x_ref, r_ref, dr_ref, colt_ref):
    def body(step, carry):
        for j in range(UNROLL // 2):
            z = step * (UNROLL // 2) + j
            for span, ref in zip(spans_of(meta, z, far_chip), refs):
                rows = ref[z]
                for s in range(SC):
                    k = slots[s, 0, span]
                    b = slots[s, 2, span]
                    x = x_ref[span, s]
                    x = jnp.where(s < counts[span], x, jnp.zeros_like(x))
                    far = lax.dot_general(x, rows, TN, preferred_element_type=F32).astype(BF16)
                    colt_ref[b] += jnp.dot(far, jnp.concatenate([r_ref[k], dr_ref[k]], axis=0),
                                           preferred_element_type=F32)
        return carry

    lax.fori_loop(0, NZ * 2 // UNROLL, body, 0)


def far_kernel_a(slots, counts, meta, r0, r1, x_ref, r_ref, dr_ref, colt_ref):
    colt_ref[...] = jnp.zeros_like(colt_ref)
    far_sums(False, slots, counts, meta, (r0, r1), x_ref, r_ref, dr_ref, colt_ref)


def far_kernel_b(slots, counts, meta, r0, r1, x_ref, r_ref, dr_ref, held_ref, colt_ref):
    colt_ref[...] = held_ref[...]
    far_sums(True, slots, counts, meta, (r0, r1), x_ref, r_ref, dr_ref, colt_ref)


def row_kernel(meta, recv_ref, total_ref, keep_ref, send_ref):
    c, xh = meta[0], meta[2]
    exps = exps_of(recv_ref[ROW_EXP:])
    merged = []
    for q in range(NQ):
        merged.append(dec(recv_ref[q * T:(q + 1) * T], exps[q:q + 1]) + total_ref[q * 2 + c])
    rows = []
    for z in range(NZ):
        a, b = merged[2 * z], merged[2 * z + 1]
        keep_ref[z] = jnp.where(xh == 0, a, b)
        val, e = enc(jnp.where(xh == 0, b, a))
        send_ref[z * T:(z + 1) * T] = val
        rows.append(e)
    send_ref[XH_EXP:] = exps_block(rows)


def merge_kernel(meta, recv_ref, core_a, core_b, colt_ref, gram_ref, after, out_ref):
    exps = exps_of(recv_ref[CORE_EXP:])
    g_hi, g_lo, g_e = enc_wide(gram_ref[...])
    start = meta[0] * HALF
    for g in range(NG):
        i, xh = g // 8 * 4 + g % 4, g // 4 % 2
        val, e0 = enc(colt_ref[i, xh * 64:(xh + 1) * 64])
        out_ref[g, 0:C1_CORE] = val
        got = dec(recv_ref[g * PIECE:(g + 1) * PIECE], exps[g:g + 1])
        at = pl.ds(pl.multiple_of(start + g * PIECE, 16), PIECE)
        val, e1 = enc(got + core_a[at] + core_b[at])
        out_ref[g, C1_CORE:C1_GRAM] = val
        out_ref[g, C1_GRAM:C1_GRAM + 16] = g_hi
        out_ref[g, C1_GRAM + 16:C1_EXP] = g_lo
        out_ref[g, C1_EXP:] = exps_block([e0, e1, g_e])


def second_kernel(meta, r1_ref, recv_ref, keep_ref, out_ref, own_ref, across_ref):
    col = [jnp.zeros((64, T), F32) for _ in range(2)]
    gram = [jnp.zeros((16, T), F32) for _ in range(2)]
    core = jnp.zeros((PIECE, T), F32)
    for g in range(NG):
        xh = g // 4 % 2
        e = exps_of(r1_ref[g, C1_EXP:])
        col[xh] = col[xh] + dec(r1_ref[g, 0:C1_CORE], e[0:1])
        core = core + dec(r1_ref[g, C1_CORE:C1_GRAM], e[1:2])
        gram[xh] = gram[xh] + dec_wide(r1_ref[g, C1_GRAM:C1_GRAM + 16], r1_ref[g, C1_GRAM + 16:C1_EXP], e[2:3])
    own_ref[...] = jnp.where(meta[2] == 0, col[0], col[1])
    across_ref[...] = jnp.where(meta[2] == 0, col[1], col[0])
    core, e1 = enc(core)
    gram, g_e = enc(jnp.concatenate(gram, axis=0))
    exps = exps_of(recv_ref[XH_EXP:])
    for z in range(NZ):
        val, e0 = enc(dec(recv_ref[z * T:(z + 1) * T], exps[z:z + 1]) + keep_ref[z])
        out_ref[z, 0:C2_CORE] = val
        out_ref[z, C2_CORE:C2_GRAM] = core
        out_ref[z, C2_GRAM:C2_EXP] = gram
        out_ref[z, C2_EXP:] = exps_block([e0, e1, g_e])


def third_kernel(meta, r2_ref, own_ref, across_ref, r_ref, dr_ref, hv_ref, out_ref, gram_s, cross_s, col_s, term_s):
    xh, off = meta[2], meta[4]
    total = jnp.zeros((T, T), F32)
    core = jnp.zeros((PIECE, T), F32)
    for z in range(NZ):
        e = exps_of(r2_ref[z, C2_EXP:])
        total = total + dec(r2_ref[z, 0:T], e[0:1])
        core = core + dec(r2_ref[z, C2_CORE:C2_GRAM], e[1:2])
        g = dec(r2_ref[z, C2_GRAM:C2_EXP], e[2:3])
        for half in range(2):
            at = (2 * z + half) * 8
            cross_s[at:at + 8] = g[half * 16:half * 16 + 8]
            gram_s[at:at + 8] = g[half * 16 + 8:half * 16 + 16]
    col_s[pl.ds(pl.multiple_of(xh * 64, 64), 64)] = own_ref[...]
    col_s[pl.ds(pl.multiple_of(64 - xh * 64, 64), 64)] = across_ref[...]
    hv_ref[...] = (-(total + col_s[...])).astype(BF16)
    gram = gram_s[...]
    cross = cross_s[...]
    d_gram = cross + cross.T
    mm = lambda a, b: jnp.dot(a, b, precision=HIGH, preferred_element_type=F32)
    for n in range(3):
        r = r_ref[n].astype(F32)
        dr = dr_ref[n].astype(F32)
        left = mm(d_gram, r) + mm(gram, dr)
        right = mm(gram, r)
        term_s[n * T:(n + 1) * T] = mm(left, gram) + mm(right, d_gram)
    val, e = enc(term_s[pl.ds(pl.multiple_of(off, 16), PIECE)] - core)
    block = exps_block([e])
    for g in range(NG):
        out_ref[g, 0:PIECE] = val
        out_ref[g, PIECE:] = block


BLOCKS = 4


def decode(ref, out_ref):
    for n in range(BLOCKS):
        e = exps_of(ref[n, PIECE:])
        out_ref[n * PIECE:(n + 1) * PIECE] = dec(ref[n, 0:PIECE], e[0:1])


def first_half(meta, ref, out_ref):
    decode(ref, out_ref)


def second_half(meta, ref, held, out_ref):
    decode(ref, out_ref)


def shape(*dims, dtype=F32):
    return jax.ShapeDtypeStruct(dims, dtype)


VM = pl.BlockSpec(memory_space=pltpu.VMEM)
SM = pl.BlockSpec(memory_space=pltpu.SMEM)
ANY = pl.BlockSpec(memory_space=pl.ANY)
HBM = pl.BlockSpec(memory_space=pltpu.HBM)
LIMIT = pltpu.CompilerParams(vmem_limit_bytes=16 * 1024 * 1024)


def call(kernel, ins, outs, *args, scratch=(), flops=0, moved=0, mib=16):
    return pl.pallas_call(
        kernel, in_specs=ins, out_specs=[VM] * len(outs), out_shape=outs, scratch_shapes=list(scratch),
        compiler_params=pltpu.CompilerParams(vmem_limit_bytes=mib * 1024 * 1024),
        cost_estimate=pl.CostEstimate(flops=flops, bytes_accessed=moved, transcendentals=0),
    )(*args)


def per_device(tile_values, tile_slots, counts, factor, d_factor, core_rel, d_core):
    swap = lambda a: lax.ppermute(a, "core", [(0, 1), (1, 0)])
    cross = lambda a: lax.ppermute(a, "xh", [(0, 1), (1, 0)])
    plane = ("xl", "xh", "y")
    exchange = lambda a, axes: lax.all_to_all(a, axes, 0, 0, tiled=True)
    c, xh, z = lax.axis_index("core"), lax.axis_index("xh"), lax.axis_index("z")
    xl, y = lax.axis_index("xl"), lax.axis_index("y")
    g = xl * 8 + xh * 4 + y
    first = c * HALF + g * PIECE
    k0 = jnp.minimum(first // T, RELS - 3)
    meta = jnp.stack([c, z * 2 + xh, xh, k0, first - k0 * T, xl, y]).astype(I32)
    slots = jnp.transpose(tile_slots[0, 0], (1, 2, 0))
    lives = counts.reshape(-1)
    tiles = tile_values.reshape(SPANS, SC, T, T)
    r_three = lax.dynamic_slice(core_rel, (k0, 0, 0), (3, T, T))
    dr_three = lax.dynamic_slice(d_core, (k0, 0, 0), (3, T, T))

    there = lambda a: lax.ppermute(a, "xl", [(0, 1), (1, 0)])
    d_there, f_there = there(d_factor), there(factor)
    pairs, pair = call(
        pair_kernel, [HBM] * 2, [shape(NZ, T, 2 * T, dtype=BF16), shape(T, 2 * T, dtype=BF16)], d_factor, factor,
        scratch=[pltpu.VMEM((T, T), BF16), pltpu.VMEM((T, T), BF16), pltpu.SemaphoreType.DMA((2,))])
    own = exchange(pairs, "z")
    two = jnp.stack([pair, jnp.concatenate([d_there, f_there], axis=1)])
    turn = lambda n: lax.ppermute(two, "y", [(i, (i + n) % 4) for i in range(4)])
    columns = (two, turn(1), turn(2), turn(3))
    own, columns = lax.optimization_barrier((own, columns))
    across = cross(own)
    beside = swap(own)

    near, total, send_row = call(
        near_kernel, [SM] * 3 + [HBM] * 3 + [VM] * 4,
        [shape(SPANS, SC, T, 2 * T, dtype=BF16), shape(SPANS, T, T), shape(ROW_EXP + 16, T, dtype=I16)],
        slots, lives, meta, tiles, core_rel, d_core, *columns,
        scratch=[pltpu.VMEM((SPANS, SC, T, T), BF16), pltpu.VMEM((RELS, T, T), BF16), pltpu.VMEM((RELS, T, T), BF16),
                 pltpu.VMEM((NR, T, 2 * T), BF16), pltpu.VMEM((16, T), F32), pltpu.SemaphoreType.DMA((STEPS + 2,))],
        flops=1600000000, moved=16000000)
    recv_row = swap(send_row)
    core_a, gram_a = call(
        core_kernel_a, [SM] * 2 + [VM] * 3, [shape(RELS * T, T), shape(T, 2 * T)],
        slots, meta, own, beside, near, flops=600000000, moved=9000000)
    across, gram_a = lax.optimization_barrier((across, gram_a))
    opposite = swap(across)
    (colt_a,) = call(
        far_kernel_a, [SM] * 3 + [VM] * 5, [shape(NR, T, T)],
        slots, lives, meta, own, beside, tiles, core_rel, d_core, flops=800000000, moved=6000000)
    keep, send_xh = call(
        row_kernel, [SM] + [VM] * 2,
        [shape(NZ, T, T), shape(XH_EXP + 16, T, dtype=I16)],
        meta, recv_row, total, flops=20000000, moved=4000000)
    recv_xh = cross(send_xh)
    core_b, send_core, gram = call(
        core_kernel_b, [SM] * 2 + [VM] * 5 + [ANY],
        [shape(RELS * T, T), shape(HALF + 16, T, dtype=I16), shape(16, T)],
        slots, meta, across, opposite, near, core_a, gram_a, send_xh,
        scratch=[pltpu.VMEM((T, 2 * T), F32), pltpu.VMEM((16, T), F32)], flops=600000000, moved=9000000)
    recv_core = swap(send_core)
    (colt,) = call(
        far_kernel_b, [SM] * 3 + [VM] * 6, [shape(NR, T, T)],
        slots, lives, meta, across, opposite, tiles, core_rel, d_core, colt_a,
        flops=800000000, moved=6000000)
    (c1,) = call(
        merge_kernel, [SM] + [VM] * 5 + [ANY], [shape(NG, C1_ROWS, T, dtype=I16)],
        meta, recv_core, core_a, core_b, colt, gram, recv_xh)
    r1 = exchange(c1, plane)
    c2, col_own, col_send = call(
        second_kernel, [SM] + [VM] * 3, [shape(NZ, C2_ROWS, T, dtype=I16), shape(64, T), shape(64, T)],
        meta, r1, recv_xh, keep)
    col_across = cross(col_send)
    r2 = exchange(c2, "z")
    hv_factor, c3 = call(
        third_kernel, [SM] + [VM] * 5, [shape(T, T, dtype=BF16), shape(NG, C3_ROWS, T, dtype=I16)],
        meta, r2, col_own, col_across, r_three, dr_three,
        scratch=[pltpu.VMEM((T, T), F32)] * 3 + [pltpu.VMEM((3 * T, T), F32)])
    mine = exchange(c3, plane)
    other = swap(mine)

    steps = NG // BLOCKS
    block = pl.BlockSpec((BLOCKS, C3_ROWS, T), lambda i, m: (i, 0, 0))
    result = shape(RELS * T, T)
    half = pl.pallas_call(
        first_half,
        grid_spec=pltpu.PrefetchScalarGridSpec(
            num_scalar_prefetch=1, grid=(steps,), in_specs=[block],
            out_specs=pl.BlockSpec((BLOCKS * PIECE, T), lambda i, m: (m[0] * steps + i, 0))),
        out_shape=result, compiler_params=LIMIT,
        cost_estimate=pl.CostEstimate(flops=2000000, bytes_accessed=3000000, transcendentals=0),
    )(meta, mine)
    hv_core = pl.pallas_call(
        second_half,
        grid_spec=pltpu.PrefetchScalarGridSpec(
            num_scalar_prefetch=1, grid=(steps,), in_specs=[block, pl.BlockSpec(memory_space=pl.ANY)],
            out_specs=pl.BlockSpec((BLOCKS * PIECE, T), lambda i, m: ((1 - m[0]) * steps + i, 0))),
        out_shape=result, input_output_aliases={2: 0}, compiler_params=LIMIT,
    )(meta, other, half)
    return hv_factor, hv_core.reshape(RELS, T, T)


def solution(mesh):
    chips = Mesh(mesh.devices.reshape(2, 4, 8, 2, 2), ("xl", "y", "z", "xh", "core"))
    row, col = ("xl", "y"), ("z", "xh", "core")
    placed = (
        P(row, col, None, None, None, None),
        P(row, col, None, None, None),
        P(row, col, None),
        P(row + col, None),
        P(row + col, None),
        P(),
        P(),
    )
    return jax.shard_map(
        per_device,
        mesh=chips,
        in_specs=placed,
        out_specs=(P(row + col, None), P()),
        check_vma=False,
    )
```

```python
import jax
import jax.numpy as jnp
from jax import lax
from jax.experimental import pallas as pl
from jax.experimental.pallas import tpu as pltpu
from jax.sharding import Mesh
from jax.sharding import PartitionSpec as P

F32 = jnp.float32
BF16 = jnp.bfloat16
I16 = jnp.int16
I32 = jnp.int32
HIGH = lax.Precision.HIGHEST

T = 128
SC = 3
SPANS = 32
NR = 8
NZ = 8
UNROLL = 8
STEPS = SPANS // UNROLL
NG = 16
NQ = 16
RELS = 60
HALF = RELS // 2 * T
PIECE = HALF // NG
ROW_EXP = NQ * T
CORE_EXP = 4 * PIECE
XH_EXP = NZ * T
C1_GRAM = PIECE
C1_EXP = C1_GRAM + 32
C1_ROWS = C1_EXP + 16
C2_CORE = T
C2_GRAM = C2_CORE + PIECE
C2_EXP = C2_GRAM + 32
C2_ROWS = C2_EXP + 16
C3_ROWS = PIECE + 16

NT = (((1,), (1,)), ((), ()))
TN = (((0,), (0,)), ((), ()))


def exponent_of(x):
    top = jnp.max(jnp.abs(x), axis=0, keepdims=True)
    e = jnp.floor(jnp.log2(jnp.maximum(top, 1e-37))) + 1.0
    return jnp.clip(e, -100.0, 127.0)


def coded(x, e):
    q = jnp.round(x * jnp.exp2(15.0 - e))
    return jnp.clip(q, -32767.0, 32767.0).astype(I32)


def enc(x):
    e = exponent_of(x)
    return coded(x, e).astype(I16), e


def enc_wide(x):
    e = exponent_of(x)
    q = x * jnp.exp2(15.0 - e)
    hi = jnp.clip(jnp.round(q), -32767.0, 32767.0)
    lo = jnp.clip(jnp.round((q - hi) * 16384.0), -32767.0, 32767.0)
    return hi.astype(I32).astype(I16), lo.astype(I32).astype(I16), e


def dec(q, e):
    return q.astype(I32).astype(F32) * jnp.exp2(e - 15.0)


def dec_wide(hi, lo, e):
    return (hi.astype(I32).astype(F32) + lo.astype(I32).astype(F32) * (1.0 / 16384.0)) * jnp.exp2(e - 15.0)


def exps_of(block):
    return block.astype(I32).astype(F32)


def exps_block(rows):
    place = lax.broadcasted_iota(I32, (16, T), 0)
    out = jnp.zeros((16, T), F32)
    for r, e in enumerate(rows):
        out = jnp.where(place == r, e, out)
    return out.astype(I32).astype(I16)


def pair_kernel(d_hbm, f_hbm, wide_ref, one_ref, d_s, f_s, sems):
    one = pltpu.make_async_copy(d_hbm, d_s, sems.at[0])
    two = pltpu.make_async_copy(f_hbm, f_s, sems.at[1])
    one.start()
    two.start()
    one.wait()
    two.wait()
    one_ref[:, 0:T] = d_s[...]
    one_ref[:, T:] = f_s[...]
    for i in range(NZ):
        wide_ref[i] = one_ref[...]


def near_kernel(table, meta, x_hbm, r_hbm, dr_hbm, c0, c1, c2, c3,
                near_ref, total_ref, send_ref, x_s, r_s, dr_s, col_s, exps, sems):
    tiles = [pltpu.make_async_copy(x_hbm.at[pl.ds(n * UNROLL, UNROLL)], x_s.at[pl.ds(n * UNROLL, UNROLL)], sems.at[n])
             for n in range(STEPS)]
    cores = [pltpu.make_async_copy(r_hbm, r_s, sems.at[STEPS]), pltpu.make_async_copy(dr_hbm, dr_s, sems.at[STEPS + 1])]
    for copy in tiles + cores:
        copy.start()
    for n, ref in enumerate((c0, c1, c2, c3)):
        col_s[2 * n] = ref[0]
        col_s[2 * n + 1] = ref[1]
    xl, y = meta[5], meta[6]

    for step in range(STEPS):
        tiles[step].wait()
        for j in range(UNROLL):
            span = step * UNROLL + j
            for s in range(SC):
                b = table[3 + s, span]
                at = ((y - b) & 3) * 2 + ((b >> 2) ^ xl)
                x = x_s[span, s]
                x = jnp.where(table[6 + s, span] > 0, x, jnp.zeros_like(x))
                near_ref[span, s] = jnp.dot(x, col_s[at], preferred_element_type=F32).astype(BF16)
    for copy in cores:
        copy.wait()

    def body(step, carry):
        for j in range(2 * UNROLL):
            span = step * 2 * UNROLL + j
            total = None
            for s in range(SC):
                k = table[s, span]
                both = jnp.concatenate([r_s[k], dr_s[k]], axis=1)
                term = lax.dot_general(near_ref[span, s], both, NT, preferred_element_type=F32)
                total = term if total is None else total + term
            total_ref[span] = total
        return carry

    lax.fori_loop(0, STEPS // 2, body, 0)

    def code(q, carry):
        val, e = enc(total_ref[q * 2 + 1 - meta[0]])
        send_ref[pl.ds(pl.multiple_of(q * T, T), T)] = val
        exps[pl.ds(q, 1)] = e
        return carry

    lax.fori_loop(0, NQ, code, 0, unroll=4)
    send_ref[ROW_EXP:] = exps[...].astype(I32).astype(I16)


def spans_of(meta, z, far_chip):
    c = meta[0]
    xh = 1 - meta[2] if far_chip else meta[2]
    return z * 4 + xh * 2 + c, z * 4 + xh * 2 + 1 - c


def core_sums(far_chip, table, meta, refs, near_ref, core_ref, gram_ref):
    core_ref[...] = jnp.zeros_like(core_ref)
    gram = jnp.zeros((T, 2 * T), F32)
    for z in range(NZ):
        for span, ref in zip(spans_of(meta, z, far_chip), refs):
            rows = ref[z]
            rows_t = rows.T
            gram = gram + jnp.dot(rows_t[T:], rows, preferred_element_type=F32)
            lhs = jnp.concatenate([rows_t[T:], rows_t[:T]], axis=1)
            for s in range(SC):
                k = table[s, span]
                near = near_ref[span, s]
                place = pl.ds(pl.multiple_of(k * T, T), T)
                core_ref[place] += jnp.dot(lhs, jnp.concatenate([near[:, :T], near[:, T:]], axis=0),
                                           preferred_element_type=F32)
    gram_ref[...] = gram


def core_kernel_a(table, meta, r0, r1, near_ref, core_ref, gram_ref):
    core_sums(False, table, meta, (r0, r1), near_ref, core_ref, gram_ref)


def core_kernel_b(table, meta, r0, r1, near_ref, held_ref, gram_held, after, core_ref, s0, s1, s2, s3, gram_out, gram_acc):
    core_sums(True, table, meta, (r0, r1), near_ref, core_ref, gram_acc)
    start = (1 - meta[0]) * HALF
    for n, send_ref in enumerate((s0, s1, s2, s3)):
        rows = []
        for g in range(4):
            at = pl.ds(pl.multiple_of(start + (n * 4 + g) * PIECE, 16), PIECE)
            val, e = enc(core_ref[at] + held_ref[at])
            send_ref[g * PIECE:(g + 1) * PIECE] = val
            rows.append(e)
        send_ref[CORE_EXP:] = exps_block(rows)
    at = pl.ds(pl.multiple_of(meta[1] * 8, 8), 8)
    part = gram_acc[at] + gram_held[at]
    gram_out[0:8] = part[:, :T]
    gram_out[8:16] = part[:, T:]


def far_sums(far_chip, table, meta, refs, x_ref, r_ref, dr_ref, colt_ref):
    for z in range(NZ):
        for span, ref in zip(spans_of(meta, z, far_chip), refs):
            rows = ref[z]
            for s in range(SC):
                k = table[s, span]
                b = table[3 + s, span]
                x = x_ref[span, s]
                x = jnp.where(table[6 + s, span] > 0, x, jnp.zeros_like(x))
                far = lax.dot_general(x, rows, TN, preferred_element_type=F32).astype(BF16)
                colt_ref[b] += jnp.dot(far, jnp.concatenate([r_ref[k], dr_ref[k]], axis=0),
                                       preferred_element_type=F32)


def far_kernel_a(table, meta, r0, r1, x_ref, r_ref, dr_ref, after, colt_ref):
    colt_ref[...] = jnp.zeros_like(colt_ref)
    far_sums(False, table, meta, (r0, r1), x_ref, r_ref, dr_ref, colt_ref)


def far_kernel_b(table, meta, r0, r1, x_ref, r_ref, dr_ref, held_ref, colt_ref):
    colt_ref[...] = held_ref[...]
    far_sums(True, table, meta, (r0, r1), x_ref, r_ref, dr_ref, colt_ref)


def row_kernel(meta, recv_ref, total_ref, keep_ref, send_ref):
    c, xh = meta[0], meta[2]
    exps = exps_of(recv_ref[ROW_EXP:])
    merged = []
    for q in range(NQ):
        merged.append(dec(recv_ref[q * T:(q + 1) * T], exps[q:q + 1]) + total_ref[q * 2 + c])
    rows = []
    for z in range(NZ):
        a, b = merged[2 * z], merged[2 * z + 1]
        keep_ref[z] = jnp.where(xh == 0, a, b)
        val, e = enc(jnp.where(xh == 0, b, a))
        send_ref[z * T:(z + 1) * T] = val
        rows.append(e)
    send_ref[XH_EXP:] = exps_block(rows)


def merge_kernel(meta, v0, v1, v2, v3, core_a, core_b, gram_ref, after, done, out_ref):
    recv = (v0, v1, v2, v3)
    exps = [exps_of(ref[CORE_EXP:]) for ref in recv]
    g_hi, g_lo, g_e = enc_wide(gram_ref[...])
    start = meta[0] * HALF
    for g in range(NG):
        n, at = g // 4, g % 4
        got = dec(recv[n][at * PIECE:(at + 1) * PIECE], exps[n][at:at + 1])
        at = pl.ds(pl.multiple_of(start + g * PIECE, 16), PIECE)
        val, e = enc(got + core_a[at] + core_b[at])
        out_ref[g, 0:C1_GRAM] = val
        out_ref[g, C1_GRAM:C1_GRAM + 16] = g_hi
        out_ref[g, C1_GRAM + 16:C1_EXP] = g_lo
        out_ref[g, C1_EXP:] = exps_block([e, g_e])


def second_kernel(r1_ref, recv_ref, keep_ref, out_ref):
    gram = [jnp.zeros((16, T), F32) for _ in range(2)]
    core = jnp.zeros((PIECE, T), F32)
    for g in range(NG):
        xh = g // 4 % 2
        e = exps_of(r1_ref[g, C1_EXP:])
        core = core + dec(r1_ref[g, 0:C1_GRAM], e[0:1])
        gram[xh] = gram[xh] + dec_wide(r1_ref[g, C1_GRAM:C1_GRAM + 16], r1_ref[g, C1_GRAM + 16:C1_EXP], e[1:2])
    core, e1 = enc(core)
    gram, g_e = enc(jnp.concatenate(gram, axis=0))
    exps = exps_of(recv_ref[XH_EXP:])
    for z in range(NZ):
        val, e0 = enc(dec(recv_ref[z * T:(z + 1) * T], exps[z:z + 1]) + keep_ref[z])
        out_ref[z, 0:C2_CORE] = val
        out_ref[z, C2_CORE:C2_GRAM] = core
        out_ref[z, C2_GRAM:C2_EXP] = gram
        out_ref[z, C2_EXP:] = exps_block([e0, e1, g_e])


def column_kernel(meta, colt_ref, after, send_ref):
    rows = []
    for y in range(4):
        val, e = enc(colt_ref[(1 - meta[5]) * 4 + y])
        send_ref[y * T:(y + 1) * T] = val
        rows.append(e)
    send_ref[4 * T:] = exps_block(rows)


def turn_kernel(meta, recv_ref, colt_ref, keep_ref, s1, s2, s3, tile_s):
    exps = exps_of(recv_ref[4 * T:])
    for y in range(4):
        tile_s[y] = dec(recv_ref[y * T:(y + 1) * T], exps[y:y + 1]) + colt_ref[meta[5] * 4 + y]
    keep_ref[...] = tile_s[meta[6]]
    for n, ref in enumerate((s1, s2, s3)):
        val, e = enc(tile_s[(meta[6] + n + 1) & 3])
        ref[0:T] = val
        ref[T:] = exps_block([e])


def parts_of(x):
    a = x.astype(BF16)
    rest = x - a.astype(F32)
    b = rest.astype(BF16)
    return [a, b, (rest - b.astype(F32)).astype(BF16)]


def third_kernel(meta, r2_ref, col_ref, t1, t2, t3, r_ref, dr_ref, hv_ref, out_ref, gram_s, cross_s, term_s):
    off = meta[4]
    total = col_ref[...]
    for ref in (t1, t2, t3):
        total = total + dec(ref[0:T], exps_of(ref[T:])[0:1])
    core = jnp.zeros((PIECE, T), F32)
    for z in range(NZ):
        e = exps_of(r2_ref[z, C2_EXP:])
        total = total + dec(r2_ref[z, 0:T], e[0:1])
        core = core + dec(r2_ref[z, C2_CORE:C2_GRAM], e[1:2])
        g = dec(r2_ref[z, C2_GRAM:C2_EXP], e[2:3])
        for half in range(2):
            at = (2 * z + half) * 8
            cross_s[at:at + 8] = g[half * 16:half * 16 + 8]
            gram_s[at:at + 8] = g[half * 16 + 8:half * 16 + 16]
    hv_ref[...] = (-total).astype(BF16)
    gram = gram_s[...]
    cross = cross_s[...]
    d_gram = cross + cross.T
    gram_parts, d_parts = parts_of(gram), parts_of(d_gram)
    lefts, rights = [], []
    for n in range(3):
        r, dr = r_ref[n], dr_ref[n]
        rows = jnp.concatenate([r, r, r, dr, dr, dr], axis=0)
        lefts.append(jnp.dot(jnp.concatenate(d_parts + gram_parts, axis=1), rows, preferred_element_type=F32))
        rights.append(jnp.dot(jnp.concatenate(gram_parts, axis=1), rows[:3 * T], preferred_element_type=F32))
    both = jnp.concatenate([jnp.concatenate(lefts, axis=0), jnp.concatenate(rights, axis=0)], axis=1)
    term_s[...] = jnp.dot(both, jnp.concatenate([gram, d_gram], axis=0), precision=HIGH, preferred_element_type=F32)
    val, e = enc(term_s[pl.ds(pl.multiple_of(off, 16), PIECE)] - core)
    block = exps_block([e])
    for g in range(NG):
        out_ref[g, 0:PIECE] = val
        out_ref[g, PIECE:] = block


BLOCKS = 8


def decode(ref, out_ref):
    for n in range(BLOCKS):
        e = exps_of(ref[n, PIECE:])
        out_ref[n * PIECE:(n + 1) * PIECE] = dec(ref[n, 0:PIECE], e[0:1])


def first_half(meta, ref, out_ref):
    decode(ref, out_ref)


def second_half(meta, ref, held, out_ref):
    decode(ref, out_ref)


def shape(*dims, dtype=F32):
    return jax.ShapeDtypeStruct(dims, dtype)


VM = pl.BlockSpec(memory_space=pltpu.VMEM)
SM = pl.BlockSpec(memory_space=pltpu.SMEM)
ANY = pl.BlockSpec(memory_space=pl.ANY)
HBM = pl.BlockSpec(memory_space=pltpu.HBM)
LIMIT = pltpu.CompilerParams(vmem_limit_bytes=16 * 1024 * 1024)


def call(kernel, ins, outs, *args, scratch=(), flops=0, moved=0, mib=16):
    return pl.pallas_call(
        kernel, in_specs=ins, out_specs=[VM] * len(outs), out_shape=outs, scratch_shapes=list(scratch),
        compiler_params=pltpu.CompilerParams(vmem_limit_bytes=mib * 1024 * 1024),
        cost_estimate=pl.CostEstimate(flops=flops, bytes_accessed=moved, transcendentals=0),
    )(*args)


def per_device(tile_values, tile_slots, counts, factor, d_factor, core_rel, d_core):
    held = lambda a: pltpu.with_memory_space_constraint(a, pltpu.HBM)
    swap = lambda a: lax.ppermute(a, "core", [(0, 1), (1, 0)])
    cross = lambda a: lax.ppermute(a, "xh", [(0, 1), (1, 0)])
    plane = ("xl", "xh", "y")
    exchange = lambda a, axes: lax.all_to_all(a, axes, 0, 0, tiled=True)
    c, xh, z = lax.axis_index("core"), lax.axis_index("xh"), lax.axis_index("z")
    xl, y = lax.axis_index("xl"), lax.axis_index("y")
    g = xl * 8 + xh * 4 + y
    first = c * HALF + g * PIECE
    k0 = jnp.minimum(first // T, RELS - 3)
    meta = jnp.stack([c, z * 2 + xh, xh, k0, first - k0 * T, xl, y]).astype(I32)
    slots = jnp.transpose(tile_slots[0, 0], (1, 2, 0))
    lives = jnp.arange(SC, dtype=I32)[:, None] < counts[0]
    table = jnp.concatenate([slots[:, 0], slots[:, 2], lives.astype(I32)])
    tiles = tile_values.reshape(SPANS, SC, T, T)
    r_three = lax.dynamic_slice(core_rel, (k0, 0, 0), (3, T, T))
    dr_three = lax.dynamic_slice(d_core, (k0, 0, 0), (3, T, T))

    over_xl = lambda a: lax.ppermute(a, "xl", [(0, 1), (1, 0)])
    d_there, f_there = over_xl(d_factor), over_xl(factor)
    pairs, pair = call(
        pair_kernel, [HBM] * 2, [shape(NZ, T, 2 * T, dtype=BF16), shape(T, 2 * T, dtype=BF16)],
        held(d_factor), held(factor),
        scratch=[pltpu.VMEM((T, T), BF16), pltpu.VMEM((T, T), BF16), pltpu.SemaphoreType.DMA((2,))])
    own = exchange(pairs, "z")
    two = jnp.stack([pair, jnp.concatenate([d_there, f_there], axis=1)])
    turn = lambda n: lax.ppermute(two, "y", [(i, (i + n) % 4) for i in range(4)])
    columns = (two, turn(1), turn(2), turn(3))
    own, columns, table, meta = lax.optimization_barrier((own, columns, table, meta))
    across = cross(own)
    beside = swap(own)

    near, total, send_row = call(
        near_kernel, [SM] * 2 + [HBM] * 3 + [VM] * 4,
        [shape(SPANS, SC, T, 2 * T, dtype=BF16), shape(SPANS, T, T), shape(ROW_EXP + 16, T, dtype=I16)],
        table, meta, held(tiles), held(core_rel), held(d_core), *columns,
        scratch=[pltpu.VMEM((SPANS, SC, T, T), BF16), pltpu.VMEM((RELS, T, T), BF16), pltpu.VMEM((RELS, T, T), BF16),
                 pltpu.VMEM((NR, T, 2 * T), BF16), pltpu.VMEM((16, T), F32), pltpu.SemaphoreType.DMA((STEPS + 2,))],
        flops=6000000000, moved=16000000)
    recv_row = swap(send_row)
    core_a, gram_a = call(
        core_kernel_a, [SM] * 2 + [VM] * 3, [shape(RELS * T, T), shape(T, 2 * T)],
        table, meta, own, beside, near, flops=2800000000, moved=9000000)
    across, gram_a = lax.optimization_barrier((across, gram_a))
    opposite = swap(across)
    keep, send_xh = call(
        row_kernel, [SM] + [VM] * 2,
        [shape(NZ, T, T), shape(XH_EXP + 16, T, dtype=I16)],
        meta, recv_row, total, flops=1000, moved=1000)
    recv_xh = cross(send_xh)
    (colt_a,) = call(
        far_kernel_a, [SM] * 2 + [VM] * 5 + [ANY], [shape(NR, T, T)],
        table, meta, own, beside, tiles, core_rel, d_core, send_xh, flops=3000000000, moved=1000)
    core_b, *send_core, gram = call(
        core_kernel_b, [SM] * 2 + [VM] * 5 + [ANY],
        [shape(RELS * T, T)] + [shape(CORE_EXP + 16, T, dtype=I16)] * 4 + [shape(16, T)],
        table, meta, across, opposite, near, core_a, gram_a, colt_a,
        scratch=[pltpu.VMEM((T, 2 * T), F32)], flops=1000, moved=1000)
    recv_core = [swap(a) for a in send_core]
    (colt,) = call(
        far_kernel_b, [SM] * 2 + [VM] * 6, [shape(NR, T, T)],
        table, meta, across, opposite, tiles, core_rel, d_core, colt_a, flops=1000, moved=1000)
    (c1,) = call(
        merge_kernel, [SM] + [VM] * 7 + [ANY] * 2, [shape(NG, C1_ROWS, T, dtype=I16)],
        meta, *recv_core, core_a, core_b, gram, recv_xh, colt, flops=1600000000, moved=8000000)
    r1 = exchange(c1, plane)
    (c2,) = call(second_kernel, [VM] * 3, [shape(NZ, C2_ROWS, T, dtype=I16)], r1, recv_xh, keep,
                 flops=1300000000, moved=4000000)
    r2 = exchange(c2, "z")
    (send_col,) = call(
        column_kernel, [SM, VM, ANY], [shape(4 * T + 16, T, dtype=I16)], meta, colt, r1, flops=600000000, moved=500000)
    col_keep, *turned = call(
        turn_kernel, [SM] + [VM] * 2, [shape(T, T)] + [shape(T + 16, T, dtype=I16)] * 3,
        meta, over_xl(send_col), colt, scratch=[pltpu.VMEM((4, T, T), F32)], flops=600000000, moved=500000)
    turned = [lax.ppermute(a, "y", [(i, (i + n + 1) % 4) for i in range(4)]) for n, a in enumerate(turned)]
    hv_factor, c3 = call(
        third_kernel, [SM] + [VM] * 7, [shape(T, T, dtype=BF16), shape(NG, C3_ROWS, T, dtype=I16)],
        meta, r2, col_keep, *turned, r_three, dr_three,
        scratch=[pltpu.VMEM((T, T), F32)] * 2 + [pltpu.VMEM((3 * T, T), F32)], flops=3000000000, moved=2000000)
    mine = exchange(c3, plane)
    other = swap(mine)

    steps = NG // BLOCKS
    block = pl.BlockSpec((BLOCKS, C3_ROWS, T), lambda i, m: (i, 0, 0))
    result = shape(RELS * T, T)
    half = pl.pallas_call(
        first_half,
        grid_spec=pltpu.PrefetchScalarGridSpec(
            num_scalar_prefetch=1, grid=(steps,), in_specs=[block],
            out_specs=pl.BlockSpec((BLOCKS * PIECE, T), lambda i, m: (m[0] * steps + i, 0))),
        out_shape=result, compiler_params=LIMIT,
        cost_estimate=pl.CostEstimate(flops=2000000, bytes_accessed=3000000, transcendentals=0),
    )(meta, mine)
    hv_core = pl.pallas_call(
        second_half,
        grid_spec=pltpu.PrefetchScalarGridSpec(
            num_scalar_prefetch=1, grid=(steps,), in_specs=[block, pl.BlockSpec(memory_space=pl.ANY)],
            out_specs=pl.BlockSpec((BLOCKS * PIECE, T), lambda i, m: ((1 - m[0]) * steps + i, 0))),
        out_shape=result, input_output_aliases={2: 0}, compiler_params=LIMIT,
    )(meta, other, half)
    return hv_factor, hv_core.reshape(RELS, T, T)


def solution(mesh):
    chips = Mesh(mesh.devices.reshape(2, 4, 8, 2, 2), ("xl", "y", "z", "xh", "core"))
    row, col = ("xl", "y"), ("z", "xh", "core")
    placed = (
        P(row, col, None, None, None, None),
        P(row, col, None, None, None),
        P(row, col, None),
        P(row + col, None),
        P(row + col, None),
        P(),
        P(),
    )
    return jax.shard_map(
        per_device,
        mesh=chips,
        in_specs=placed,
        out_specs=(P(row + col, None), P()),
        check_vma=False,
    )
```

```python
import jax
import jax.numpy as jnp
from jax import lax
from jax.experimental import pallas as pl
from jax.experimental.pallas import tpu as pltpu
from jax.sharding import Mesh
from jax.sharding import PartitionSpec as P

F32 = jnp.float32
BF16 = jnp.bfloat16
I16 = jnp.int16
I32 = jnp.int32
HIGH = lax.Precision.HIGHEST

T = 128
SC = 3
SPANS = 32
NR = 8
NZ = 8
UNROLL = 8
STEPS = SPANS // UNROLL
NG = 16
NQ = 16
RELS = 60
HALF = RELS // 2 * T
PIECE = HALF // NG
ROW_EXP = NQ * T
CORE_EXP = 4 * PIECE
XH_EXP = NZ * T
C1_GRAM = PIECE
C1_EXP = C1_GRAM + 16
C1_ROWS = C1_EXP + 16
C2_CORE = T
C2_GRAM = C2_CORE + PIECE
C2_EXP = C2_GRAM + 32
C2_ROWS = C2_EXP + 16
C3_ROWS = PIECE + 16

NT = (((1,), (1,)), ((), ()))
TN = (((0,), (0,)), ((), ()))


def exponent_of(x):
    top = jnp.max(jnp.abs(x), axis=0, keepdims=True)
    e = jnp.floor(jnp.log2(jnp.maximum(top, 1e-37))) + 1.0
    return jnp.clip(e, -100.0, 127.0)


def coded(x, e):
    q = jnp.round(x * jnp.exp2(15.0 - e))
    return jnp.clip(q, -32767.0, 32767.0).astype(I32)


def enc(x):
    e = exponent_of(x)
    return coded(x, e).astype(I16), e


def dec(q, e):
    return q.astype(I32).astype(F32) * jnp.exp2(e - 15.0)


def exps_of(block):
    return block.astype(I32).astype(F32)


def exps_block(rows):
    place = lax.broadcasted_iota(I32, (16, T), 0)
    out = jnp.zeros((16, T), F32)
    for r, e in enumerate(rows):
        out = jnp.where(place == r, e, out)
    return out.astype(I32).astype(I16)


def pair_kernel(d_hbm, f_hbm, wide_ref, one_ref, d_s, f_s, sems):
    one = pltpu.make_async_copy(d_hbm, d_s, sems.at[0])
    two = pltpu.make_async_copy(f_hbm, f_s, sems.at[1])
    one.start()
    two.start()
    one.wait()
    two.wait()
    one_ref[:, 0:T] = d_s[...]
    one_ref[:, T:] = f_s[...]
    for i in range(NZ):
        wide_ref[i] = one_ref[...]


def near_kernel(table, meta, x_hbm, r_hbm, dr_hbm, c0, c1, c2, c3,
                near_ref, total_ref, send_ref, x_s, r_s, dr_s, col_s, exps, sems):
    tiles = [pltpu.make_async_copy(x_hbm.at[pl.ds(n * UNROLL, UNROLL)], x_s.at[pl.ds(n * UNROLL, UNROLL)], sems.at[n])
             for n in range(STEPS)]
    cores = [pltpu.make_async_copy(r_hbm, r_s, sems.at[STEPS]), pltpu.make_async_copy(dr_hbm, dr_s, sems.at[STEPS + 1])]
    for copy in tiles + cores:
        copy.start()
    for n, ref in enumerate((c0, c1, c2, c3)):
        col_s[2 * n] = ref[0]
        col_s[2 * n + 1] = ref[1]
    xl, y = meta[5], meta[6]

    for step in range(STEPS):
        tiles[step].wait()
        for j in range(UNROLL):
            span = step * UNROLL + j
            for s in range(SC):
                b = table[3 + s, span]
                at = ((y - b) & 3) * 2 + ((b >> 2) ^ xl)
                x = x_s[span, s]
                x = jnp.where(table[6 + s, span] > 0, x, jnp.zeros_like(x))
                near_ref[span, s] = jnp.dot(x, col_s[at], preferred_element_type=F32).astype(BF16)
    for copy in cores:
        copy.wait()

    for span in range(SPANS):
        total = None
        for s in range(SC):
            k = table[s, span]
            both = jnp.concatenate([r_s[k], dr_s[k]], axis=1)
            term = lax.dot_general(near_ref[span, s], both, NT, preferred_element_type=F32)
            total = term if total is None else total + term
        total_ref[span] = total

    def code(q, carry):
        val, e = enc(total_ref[q * 2 + 1 - meta[0]])
        send_ref[pl.ds(pl.multiple_of(q * T, T), T)] = val
        exps[pl.ds(q, 1)] = e
        return carry

    lax.fori_loop(0, NQ, code, 0, unroll=4)
    send_ref[ROW_EXP:] = exps[...].astype(I32).astype(I16)


def spans_of(meta, z, far_chip):
    c = meta[0]
    xh = 1 - meta[2] if far_chip else meta[2]
    return z * 4 + xh * 2 + c, z * 4 + xh * 2 + 1 - c


def core_sums(far_chip, table, meta, refs, near_ref, core_ref, gram_ref):
    core_ref[...] = jnp.zeros_like(core_ref)
    gram = jnp.zeros((T, 2 * T), F32)
    for z in range(NZ):
        for span, ref in zip(spans_of(meta, z, far_chip), refs):
            rows = ref[z]
            rows_t = rows.T
            gram = gram + jnp.dot(rows_t[T:], rows, preferred_element_type=F32)
            lhs = jnp.concatenate([rows_t[T:], rows_t[:T]], axis=1)
            near = [near_ref[span, s] for s in range(SC)]
            near = jnp.concatenate([jnp.concatenate([n[:, :T] for n in near], axis=1),
                                    jnp.concatenate([n[:, T:] for n in near], axis=1)], axis=0)
            terms = jnp.dot(lhs, near, preferred_element_type=F32)
            for s in range(SC):
                place = pl.ds(pl.multiple_of(table[s, span] * T, T), T)
                core_ref[place] += terms[:, s * T:(s + 1) * T]
    gram_ref[...] = gram


def core_kernel_a(table, meta, r0, r1, near_ref, core_ref, gram_ref):
    core_sums(False, table, meta, (r0, r1), near_ref, core_ref, gram_ref)


def core_kernel_b(table, meta, r0, r1, near_ref, held_ref, gram_held, after, core_ref, s0, s1, s2, s3, gram_out, gram_acc):
    core_sums(True, table, meta, (r0, r1), near_ref, core_ref, gram_acc)
    start = (1 - meta[0]) * HALF
    for n, send_ref in enumerate((s0, s1, s2, s3)):
        rows = []
        for g in range(4):
            at = pl.ds(pl.multiple_of(start + (n * 4 + g) * PIECE, 16), PIECE)
            val, e = enc(core_ref[at] + held_ref[at])
            send_ref[g * PIECE:(g + 1) * PIECE] = val
            rows.append(e)
        send_ref[CORE_EXP:] = exps_block(rows)
    at = pl.ds(pl.multiple_of(meta[1] * 8, 8), 8)
    part = gram_acc[at] + gram_held[at]
    gram_out[0:8] = part[:, :T]
    gram_out[8:16] = part[:, T:]


def far_sums(far_chip, table, meta, refs, x_ref, r_ref, dr_ref, colt_ref):
    for z in range(NZ):
        for span, ref in zip(spans_of(meta, z, far_chip), refs):
            x = [x_ref[span, s] for s in range(SC)]
            x = [jnp.where(table[6 + s, span] > 0, x[s], jnp.zeros_like(x[s])) for s in range(SC)]
            far = lax.dot_general(jnp.concatenate(x, axis=1), ref[z], TN, preferred_element_type=F32).astype(BF16)
            for s in range(SC):
                k = table[s, span]
                colt_ref[table[3 + s, span]] += jnp.dot(
                    far[s * T:(s + 1) * T], jnp.concatenate([r_ref[k], dr_ref[k]], axis=0), preferred_element_type=F32)


def far_kernel_a(table, meta, r0, r1, x_ref, r_ref, dr_ref, after, colt_ref):
    colt_ref[...] = jnp.zeros_like(colt_ref)
    far_sums(False, table, meta, (r0, r1), x_ref, r_ref, dr_ref, colt_ref)


def far_kernel_b(table, meta, r0, r1, x_ref, r_ref, dr_ref, held_ref, colt_ref):
    colt_ref[...] = held_ref[...]
    far_sums(True, table, meta, (r0, r1), x_ref, r_ref, dr_ref, colt_ref)


def row_kernel(meta, recv_ref, total_ref, keep_ref, send_ref):
    c, xh = meta[0], meta[2]
    exps = exps_of(recv_ref[ROW_EXP:])
    merged = []
    for q in range(NQ):
        merged.append(dec(recv_ref[q * T:(q + 1) * T], exps[q:q + 1]) + total_ref[q * 2 + c])
    rows = []
    for z in range(NZ):
        a, b = merged[2 * z], merged[2 * z + 1]
        keep_ref[z] = jnp.where(xh == 0, a, b)
        val, e = enc(jnp.where(xh == 0, b, a))
        send_ref[z * T:(z + 1) * T] = val
        rows.append(e)
    send_ref[XH_EXP:] = exps_block(rows)


def merge_kernel(meta, v0, v1, v2, v3, core_a, core_b, gram_ref, after, done, out_ref):
    recv = (v0, v1, v2, v3)
    exps = [exps_of(ref[CORE_EXP:]) for ref in recv]
    gram, g_e = enc(gram_ref[...])
    start = meta[0] * HALF
    for g in range(NG):
        n, at = g // 4, g % 4
        got = dec(recv[n][at * PIECE:(at + 1) * PIECE], exps[n][at:at + 1])
        at = pl.ds(pl.multiple_of(start + g * PIECE, 16), PIECE)
        val, e = enc(got + core_a[at] + core_b[at])
        out_ref[g, 0:C1_GRAM] = val
        out_ref[g, C1_GRAM:C1_EXP] = gram
        out_ref[g, C1_EXP:] = exps_block([e, g_e])


def second_kernel(r1_ref, recv_ref, keep_ref, out_ref, token_ref):
    gram = [jnp.zeros((16, T), F32) for _ in range(2)]
    core = jnp.zeros((PIECE, T), F32)
    for g in range(NG):
        xh = g // 4 % 2
        e = exps_of(r1_ref[g, C1_EXP:])
        core = core + dec(r1_ref[g, 0:C1_GRAM], e[0:1])
        gram[xh] = gram[xh] + dec(r1_ref[g, C1_GRAM:C1_EXP], e[1:2])
    core, e1 = enc(core)
    gram, g_e = enc(jnp.concatenate(gram, axis=0))
    exps = exps_of(recv_ref[XH_EXP:])
    token_ref[...] = jnp.zeros_like(token_ref)
    for z in range(NZ):
        val, e0 = enc(dec(recv_ref[z * T:(z + 1) * T], exps[z:z + 1]) + keep_ref[z])
        out_ref[z, 0:C2_CORE] = val
        out_ref[z, C2_CORE:C2_GRAM] = core
        out_ref[z, C2_GRAM:C2_EXP] = gram
        out_ref[z, C2_EXP:] = exps_block([e0, e1, g_e])


def column_kernel(meta, colt_ref, after, send_ref):
    rows = []
    for y in range(4):
        val, e = enc(colt_ref[(1 - meta[5]) * 4 + y])
        send_ref[y * T:(y + 1) * T] = val
        rows.append(e)
    send_ref[4 * T:] = exps_block(rows)


def turn_kernel(meta, recv_ref, colt_ref, keep_ref, s1, s2, s3, tile_s):
    exps = exps_of(recv_ref[4 * T:])
    for y in range(4):
        tile_s[y] = dec(recv_ref[y * T:(y + 1) * T], exps[y:y + 1]) + colt_ref[meta[5] * 4 + y]
    keep_ref[...] = tile_s[meta[6]]
    for n, ref in enumerate((s1, s2, s3)):
        val, e = enc(tile_s[(meta[6] + n + 1) & 3])
        ref[0:T] = val
        ref[T:] = exps_block([e])


def parts_of(x):
    a = x.astype(BF16)
    rest = x - a.astype(F32)
    b = rest.astype(BF16)
    return [a, b, (rest - b.astype(F32)).astype(BF16)]


def third_kernel(meta, r2_ref, col_ref, t1, t2, t3, r_ref, dr_ref, hv_ref, out_ref, gram_s, cross_s, term_s):
    off = meta[4]
    total = col_ref[...]
    for ref in (t1, t2, t3):
        total = total + dec(ref[0:T], exps_of(ref[T:])[0:1])
    core = jnp.zeros((PIECE, T), F32)
    for z in range(NZ):
        e = exps_of(r2_ref[z, C2_EXP:])
        total = total + dec(r2_ref[z, 0:T], e[0:1])
        core = core + dec(r2_ref[z, C2_CORE:C2_GRAM], e[1:2])
        g = dec(r2_ref[z, C2_GRAM:C2_EXP], e[2:3])
        for half in range(2):
            at = (2 * z + half) * 8
            cross_s[at:at + 8] = g[half * 16:half * 16 + 8]
            gram_s[at:at + 8] = g[half * 16 + 8:half * 16 + 16]
    hv_ref[...] = (-total).astype(BF16)
    gram = gram_s[...]
    cross = cross_s[...]
    d_gram = cross + cross.T
    gram_parts, d_parts = parts_of(gram), parts_of(d_gram)
    lefts, rights = [], []
    for n in range(3):
        r, dr = r_ref[n], dr_ref[n]
        rows = jnp.concatenate([r, r, r, dr, dr, dr], axis=0)
        lefts.append(jnp.dot(jnp.concatenate(d_parts + gram_parts, axis=1), rows, preferred_element_type=F32))
        rights.append(jnp.dot(jnp.concatenate(gram_parts, axis=1), rows[:3 * T], preferred_element_type=F32))
    both = jnp.concatenate([jnp.concatenate(lefts, axis=0), jnp.concatenate(rights, axis=0)], axis=1)
    term_s[...] = jnp.dot(both, jnp.concatenate([gram, d_gram], axis=0), precision=HIGH, preferred_element_type=F32)
    val, e = enc(term_s[pl.ds(pl.multiple_of(off, 16), PIECE)] - core)
    block = exps_block([e])
    for g in range(NG):
        out_ref[g, 0:PIECE] = val
        out_ref[g, PIECE:] = block


STORES = 8


def decode(half, ref, out_hbm, buf, sems):
    copies = []
    for n in range(STORES):
        for g in range(n * NG // STORES, (n + 1) * NG // STORES):
            e = exps_of(ref[g, PIECE:])
            buf[g * PIECE:(g + 1) * PIECE] = dec(ref[g, 0:PIECE], e[0:1])
        rows = HALF // STORES
        to = pl.ds(pl.multiple_of(half * HALF + n * rows, 32), rows)
        copies.append(pltpu.make_async_copy(buf.at[pl.ds(n * rows, rows)], out_hbm.at[to], sems.at[n]))
        copies[n].start()
    for copy in copies:
        copy.wait()


def first_half(meta, ref, out_hbm, buf, sems):
    decode(meta[0], ref, out_hbm, buf, sems)


def second_half(meta, ref, before, out_hbm, buf, sems):
    decode(1 - meta[0], ref, out_hbm, buf, sems)


def shape(*dims, dtype=F32):
    return jax.ShapeDtypeStruct(dims, dtype)


VM = pl.BlockSpec(memory_space=pltpu.VMEM)
SM = pl.BlockSpec(memory_space=pltpu.SMEM)
ANY = pl.BlockSpec(memory_space=pl.ANY)
HBM = pl.BlockSpec(memory_space=pltpu.HBM)


def call(kernel, ins, outs, *args, scratch=(), flops=0, moved=0, space=None, alias=None):
    return pl.pallas_call(
        kernel, in_specs=ins, out_specs=[space or VM] * len(outs), out_shape=outs, scratch_shapes=list(scratch),
        input_output_aliases=alias or {},
        compiler_params=pltpu.CompilerParams(vmem_limit_bytes=16 * 1024 * 1024),
        cost_estimate=pl.CostEstimate(flops=flops, bytes_accessed=moved, transcendentals=0),
    )(*args)


def per_device(tile_values, tile_slots, counts, factor, d_factor, core_rel, d_core):
    held = lambda a: pltpu.with_memory_space_constraint(a, pltpu.HBM)
    swap = lambda a: lax.ppermute(a, "core", [(0, 1), (1, 0)])
    cross = lambda a: lax.ppermute(a, "xh", [(0, 1), (1, 0)])
    plane = ("xl", "xh", "y")
    exchange = lambda a, axes: lax.all_to_all(a, axes, 0, 0, tiled=True)
    c, xh, z = lax.axis_index("core"), lax.axis_index("xh"), lax.axis_index("z")
    xl, y = lax.axis_index("xl"), lax.axis_index("y")
    g = xl * 8 + xh * 4 + y
    first = c * HALF + g * PIECE
    k0 = jnp.minimum(first // T, RELS - 3)
    meta = jnp.stack([c, z * 2 + xh, xh, k0, first - k0 * T, xl, y]).astype(I32)
    slots = jnp.transpose(tile_slots[0, 0], (1, 2, 0))
    lives = jnp.arange(SC, dtype=I32)[:, None] < counts[0]
    table = jnp.concatenate([slots[:, 0], slots[:, 2], lives.astype(I32)])
    tiles = tile_values.reshape(SPANS, SC, T, T)
    r_three = lax.dynamic_slice(core_rel, (k0, 0, 0), (3, T, T))
    dr_three = lax.dynamic_slice(d_core, (k0, 0, 0), (3, T, T))

    over_xl = lambda a: lax.ppermute(a, "xl", [(0, 1), (1, 0)])
    d_there, f_there = over_xl(d_factor), over_xl(factor)
    pairs, pair = call(
        pair_kernel, [HBM] * 2, [shape(NZ, T, 2 * T, dtype=BF16), shape(T, 2 * T, dtype=BF16)],
        held(d_factor), held(factor),
        scratch=[pltpu.VMEM((T, T), BF16), pltpu.VMEM((T, T), BF16), pltpu.SemaphoreType.DMA((2,))])
    own = exchange(pairs, "z")
    two = jnp.stack([pair, jnp.concatenate([d_there, f_there], axis=1)])
    turn = lambda n: lax.ppermute(two, "y", [(i, (i + n) % 4) for i in range(4)])
    columns = (two, turn(1), turn(2), turn(3))
    own, columns, table, meta = lax.optimization_barrier((own, columns, table, meta))
    across = cross(own)
    beside = swap(own)

    near, total, send_row = call(
        near_kernel, [SM] * 2 + [HBM] * 3 + [VM] * 4,
        [shape(SPANS, SC, T, 2 * T, dtype=BF16), shape(SPANS, T, T), shape(ROW_EXP + 16, T, dtype=I16)],
        table, meta, held(tiles), held(core_rel), held(d_core), *columns,
        scratch=[pltpu.VMEM((SPANS, SC, T, T), BF16), pltpu.VMEM((RELS, T, T), BF16), pltpu.VMEM((RELS, T, T), BF16),
                 pltpu.VMEM((NR, T, 2 * T), BF16), pltpu.VMEM((16, T), F32), pltpu.SemaphoreType.DMA((STEPS + 2,))],
        flops=6000000000, moved=16000000)
    recv_row = swap(send_row)
    core_a, gram_a = call(
        core_kernel_a, [SM] * 2 + [VM] * 3, [shape(RELS * T, T), shape(T, 2 * T)],
        table, meta, own, beside, near, flops=2800000000, moved=9000000)
    across, gram_a = lax.optimization_barrier((across, gram_a))
    opposite = swap(across)
    keep, send_xh = call(
        row_kernel, [SM] + [VM] * 2,
        [shape(NZ, T, T), shape(XH_EXP + 16, T, dtype=I16)],
        meta, recv_row, total, flops=1000, moved=1000)
    recv_xh = cross(send_xh)
    (colt_a,) = call(
        far_kernel_a, [SM] * 2 + [VM] * 5 + [ANY], [shape(NR, T, T)],
        table, meta, own, beside, tiles, core_rel, d_core, send_xh, flops=3000000000, moved=1000)
    core_b, *send_core, gram = call(
        core_kernel_b, [SM] * 2 + [VM] * 5 + [ANY],
        [shape(RELS * T, T)] + [shape(CORE_EXP + 16, T, dtype=I16)] * 4 + [shape(16, T)],
        table, meta, across, opposite, near, core_a, gram_a, colt_a,
        scratch=[pltpu.VMEM((T, 2 * T), F32)], flops=1000, moved=1000)
    recv_core = [swap(a) for a in send_core]
    (colt,) = call(
        far_kernel_b, [SM] * 2 + [VM] * 6, [shape(NR, T, T)],
        table, meta, across, opposite, tiles, core_rel, d_core, colt_a, flops=1000, moved=1000)
    (c1,) = call(
        merge_kernel, [SM] + [VM] * 7 + [ANY] * 2, [shape(NG, C1_ROWS, T, dtype=I16)],
        meta, *recv_core, core_a, core_b, gram, recv_xh, colt, flops=1600000000, moved=8000000)
    r1 = exchange(c1, plane)
    c2, token = call(second_kernel, [VM] * 3, [shape(NZ, C2_ROWS, T, dtype=I16), shape(8, T)], r1, recv_xh, keep,
                 flops=1300000000, moved=4000000)
    r2 = exchange(c2, "z")
    (send_col,) = call(
        column_kernel, [SM, VM, ANY], [shape(4 * T + 16, T, dtype=I16)], meta, colt, r1, flops=600000000, moved=500000)
    col_keep, *turned = call(
        turn_kernel, [SM] + [VM] * 2, [shape(T, T)] + [shape(T + 16, T, dtype=I16)] * 3,
        meta, over_xl(send_col), colt, scratch=[pltpu.VMEM((4, T, T), F32)], flops=600000000, moved=500000)
    turned = [lax.ppermute(a, "y", [(i, (i + n + 1) % 4) for i in range(4)]) for n, a in enumerate(turned)]
    hv_factor, c3 = call(
        third_kernel, [SM] + [VM] * 7, [shape(T, T, dtype=BF16), shape(NG, C3_ROWS, T, dtype=I16)],
        meta, r2, col_keep, *turned, r_three, dr_three,
        scratch=[pltpu.VMEM((T, T), F32)] * 2 + [pltpu.VMEM((3 * T, T), F32)], flops=3000000000, moved=2000000)
    mine = exchange(c3, plane)
    other = swap(mine)

    result = shape(RELS * T, T)
    stores = [pltpu.VMEM((HALF, T), F32), pltpu.SemaphoreType.DMA((STORES,))]
    (half,) = call(first_half, [SM, VM], [result], meta, mine, scratch=stores, flops=2000000, moved=3000000, space=HBM)
    (hv_core,) = call(second_half, [SM, VM, HBM], [result], meta, other, half, scratch=stores, space=HBM, alias={2: 0})
    return hv_factor, hv_core.reshape(RELS, T, T)


def solution(mesh):
    chips = Mesh(mesh.devices.reshape(2, 4, 8, 2, 2), ("xl", "y", "z", "xh", "core"))
    row, col = ("xl", "y"), ("z", "xh", "core")
    placed = (
        P(row, col, None, None, None, None),
        P(row, col, None, None, None),
        P(row, col, None),
        P(row + col, None),
        P(row + col, None),
        P(),
        P(),
    )
    return jax.shard_map(
        per_device,
        mesh=chips,
        in_specs=placed,
        out_specs=(P(row + col, None), P()),
        check_vma=False,
    )
```

```python
import jax
import jax.numpy as jnp
from jax import lax
from jax.experimental import pallas as pl
from jax.experimental.pallas import tpu as pltpu
from jax.sharding import Mesh
from jax.sharding import PartitionSpec as P

F32 = jnp.float32
BF16 = jnp.bfloat16
I16 = jnp.int16
I32 = jnp.int32
HIGH = lax.Precision.HIGHEST

T = 128
SC = 3
SPANS = 32
NR = 8
NZ = 8
UNROLL = 8
STEPS = SPANS // UNROLL
NG = 16
NQ = 16
RELS = 60
HALF = RELS // 2 * T
PIECE = HALF // NG
ROW_EXP = 4 * T
CORE_EXP = 4 * PIECE
XH_EXP = NZ * T
C1_GRAM = PIECE
C1_EXP = C1_GRAM + 16
C1_ROWS = C1_EXP + 16
C2_CORE = T
C2_GRAM = C2_CORE + PIECE
C2_EXP = C2_GRAM + 32
C2_ROWS = C2_EXP + 16
C3_ROWS = PIECE + 16

NT = (((1,), (1,)), ((), ()))
TN = (((0,), (0,)), ((), ()))


def exponent_of(x):
    top = jnp.max(jnp.abs(x), axis=0, keepdims=True)
    e = jnp.floor(jnp.log2(jnp.maximum(top, 1e-37))) + 1.0
    return jnp.clip(e, -100.0, 127.0)


def coded(x, e):
    q = jnp.round(x * jnp.exp2(15.0 - e))
    return jnp.clip(q, -32767.0, 32767.0).astype(I32)


def enc(x):
    e = exponent_of(x)
    return coded(x, e).astype(I16), e


def dec(q, e):
    return q.astype(I32).astype(F32) * jnp.exp2(e - 15.0)


def exps_of(block):
    return block.astype(I32).astype(F32)


def exps_block(rows):
    place = lax.broadcasted_iota(I32, (16, T), 0)
    out = jnp.zeros((16, T), F32)
    for r, e in enumerate(rows):
        out = jnp.where(place == r, e, out)
    return out.astype(I32).astype(I16)


def pair_kernel(d_hbm, f_hbm, wide_ref, one_ref, d_s, f_s, sems):
    one = pltpu.make_async_copy(d_hbm, d_s, sems.at[0])
    two = pltpu.make_async_copy(f_hbm, f_s, sems.at[1])
    one.start()
    two.start()
    one.wait()
    two.wait()
    one_ref[:, 0:T] = d_s[...]
    one_ref[:, T:] = f_s[...]
    for i in range(NZ):
        wide_ref[i] = one_ref[...]


def near_kernel(table, meta, x_hbm, r_hbm, dr_hbm, c0, c1, c2, c3,
                near_ref, total_ref, s0, s1, s2, s3, x_s, r_s, dr_s, col_s, sems):
    tiles = [pltpu.make_async_copy(x_hbm.at[pl.ds(n * UNROLL, UNROLL)], x_s.at[pl.ds(n * UNROLL, UNROLL)], sems.at[n])
             for n in range(STEPS)]
    cores = [pltpu.make_async_copy(r_hbm, r_s, sems.at[STEPS]), pltpu.make_async_copy(dr_hbm, dr_s, sems.at[STEPS + 1])]
    for copy in tiles + cores:
        copy.start()
    for n, ref in enumerate((c0, c1, c2, c3)):
        col_s[2 * n] = ref[0]
        col_s[2 * n + 1] = ref[1]
    xl, y = meta[5], meta[6]

    for step in range(STEPS):
        tiles[step].wait()
        for j in range(UNROLL):
            span = step * UNROLL + j
            for s in range(SC):
                b = table[3 + s, span]
                at = ((y - b) & 3) * 2 + ((b >> 2) ^ xl)
                x = x_s[span, s]
                x = jnp.where(table[6 + s, span] > 0, x, jnp.zeros_like(x))
                near_ref[span, s] = jnp.dot(x, col_s[at], preferred_element_type=F32).astype(BF16)
    for copy in cores:
        copy.wait()

    for span in range(SPANS):
        total = None
        for s in range(SC):
            k = table[s, span]
            both = jnp.concatenate([r_s[k], dr_s[k]], axis=1)
            term = lax.dot_general(near_ref[span, s], both, NT, preferred_element_type=F32)
            total = term if total is None else total + term
        total_ref[span] = total

    for n, send_ref in enumerate((s0, s1, s2, s3)):
        rows = []
        for q in range(4):
            val, e = enc(total_ref[(n * 4 + q) * 2 + 1 - meta[0]])
            send_ref[q * T:(q + 1) * T] = val
            rows.append(e)
        send_ref[ROW_EXP:] = exps_block(rows)


def spans_of(meta, z, far_chip):
    c = meta[0]
    xh = 1 - meta[2] if far_chip else meta[2]
    return z * 4 + xh * 2 + c, z * 4 + xh * 2 + 1 - c


def core_sums(far_chip, table, meta, refs, near_ref, core_ref, gram_ref):
    core_ref[...] = jnp.zeros_like(core_ref)
    gram = jnp.zeros((T, 2 * T), F32)
    for z in range(NZ):
        for span, ref in zip(spans_of(meta, z, far_chip), refs):
            rows = ref[z]
            rows_t = rows.T
            gram = gram + jnp.dot(rows_t[T:], rows, preferred_element_type=F32)
            lhs = jnp.concatenate([rows_t[T:], rows_t[:T]], axis=1)
            near = [near_ref[span, s] for s in range(SC)]
            near = jnp.concatenate([jnp.concatenate([n[:, :T] for n in near], axis=1),
                                    jnp.concatenate([n[:, T:] for n in near], axis=1)], axis=0)
            terms = jnp.dot(lhs, near, preferred_element_type=F32)
            for s in range(SC):
                place = pl.ds(pl.multiple_of(table[s, span] * T, T), T)
                core_ref[place] += terms[:, s * T:(s + 1) * T]
    gram_ref[...] = gram


def core_kernel_a(table, meta, r0, r1, near_ref, core_ref, gram_ref):
    core_sums(False, table, meta, (r0, r1), near_ref, core_ref, gram_ref)


def core_kernel_b(table, meta, r0, r1, near_ref, held_ref, gram_held, after, core_ref, s0, s1, s2, s3, gram_out, gram_acc):
    core_sums(True, table, meta, (r0, r1), near_ref, core_ref, gram_acc)
    start = (1 - meta[0]) * HALF
    for n, send_ref in enumerate((s0, s1, s2, s3)):
        rows = []
        for g in range(4):
            at = pl.ds(pl.multiple_of(start + (n * 4 + g) * PIECE, 16), PIECE)
            val, e = enc(core_ref[at] + held_ref[at])
            send_ref[g * PIECE:(g + 1) * PIECE] = val
            rows.append(e)
        send_ref[CORE_EXP:] = exps_block(rows)
    at = pl.ds(pl.multiple_of(meta[1] * 8, 8), 8)
    part = gram_acc[at] + gram_held[at]
    gram_out[0:8] = part[:, :T]
    gram_out[8:16] = part[:, T:]


def far_sums(far_chip, table, meta, refs, x_ref, r_ref, dr_ref, colt_ref):
    for z in range(NZ):
        for span, ref in zip(spans_of(meta, z, far_chip), refs):
            x = [x_ref[span, s] for s in range(SC)]
            x = [jnp.where(table[6 + s, span] > 0, x[s], jnp.zeros_like(x[s])) for s in range(SC)]
            far = lax.dot_general(jnp.concatenate(x, axis=1), ref[z], TN, preferred_element_type=F32).astype(BF16)
            for s in range(SC):
                k = table[s, span]
                colt_ref[table[3 + s, span]] += jnp.dot(
                    far[s * T:(s + 1) * T], jnp.concatenate([r_ref[k], dr_ref[k]], axis=0), preferred_element_type=F32)


def far_kernel_a(table, meta, r0, r1, x_ref, r_ref, dr_ref, after, colt_ref):
    colt_ref[...] = jnp.zeros_like(colt_ref)
    far_sums(False, table, meta, (r0, r1), x_ref, r_ref, dr_ref, colt_ref)


def far_kernel_b(table, meta, r0, r1, x_ref, r_ref, dr_ref, held_ref, colt_ref):
    colt_ref[...] = held_ref[...]
    far_sums(True, table, meta, (r0, r1), x_ref, r_ref, dr_ref, colt_ref)


def row_kernel(meta, v0, v1, v2, v3, total_ref, after, keep_ref, send_ref):
    c, xh = meta[0], meta[2]
    recv = (v0, v1, v2, v3)
    exps = [exps_of(ref[ROW_EXP:]) for ref in recv]
    merged = []
    for q in range(NQ):
        n, at = q // 4, q % 4
        merged.append(dec(recv[n][at * T:(at + 1) * T], exps[n][at:at + 1]) + total_ref[q * 2 + c])
    rows = []
    for z in range(NZ):
        a, b = merged[2 * z], merged[2 * z + 1]
        keep_ref[z] = jnp.where(xh == 0, a, b)
        val, e = enc(jnp.where(xh == 0, b, a))
        send_ref[z * T:(z + 1) * T] = val
        rows.append(e)
    send_ref[XH_EXP:] = exps_block(rows)


def merge_kernel(meta, v0, v1, v2, v3, core_a, core_b, gram_ref, after, done, out_ref):
    recv = (v0, v1, v2, v3)
    exps = [exps_of(ref[CORE_EXP:]) for ref in recv]
    gram, g_e = enc(gram_ref[...])
    start = meta[0] * HALF
    for g in range(NG):
        n, at = g // 4, g % 4
        got = dec(recv[n][at * PIECE:(at + 1) * PIECE], exps[n][at:at + 1])
        at = pl.ds(pl.multiple_of(start + g * PIECE, 16), PIECE)
        val, e = enc(got + core_a[at] + core_b[at])
        out_ref[g, 0:C1_GRAM] = val
        out_ref[g, C1_GRAM:C1_EXP] = gram
        out_ref[g, C1_EXP:] = exps_block([e, g_e])


def second_kernel(r1_ref, recv_ref, keep_ref, out_ref, token_ref):
    gram = [jnp.zeros((16, T), F32) for _ in range(2)]
    core = jnp.zeros((PIECE, T), F32)
    for g in range(NG):
        xh = g // 4 % 2
        e = exps_of(r1_ref[g, C1_EXP:])
        core = core + dec(r1_ref[g, 0:C1_GRAM], e[0:1])
        gram[xh] = gram[xh] + dec(r1_ref[g, C1_GRAM:C1_EXP], e[1:2])
    core, e1 = enc(core)
    gram, g_e = enc(jnp.concatenate(gram, axis=0))
    exps = exps_of(recv_ref[XH_EXP:])
    token_ref[...] = jnp.zeros_like(token_ref)
    for z in range(NZ):
        val, e0 = enc(dec(recv_ref[z * T:(z + 1) * T], exps[z:z + 1]) + keep_ref[z])
        out_ref[z, 0:C2_CORE] = val
        out_ref[z, C2_CORE:C2_GRAM] = core
        out_ref[z, C2_GRAM:C2_EXP] = gram
        out_ref[z, C2_EXP:] = exps_block([e0, e1, g_e])


def column_kernel(meta, colt_ref, after, send_ref):
    rows = []
    for y in range(4):
        val, e = enc(colt_ref[(1 - meta[5]) * 4 + y])
        send_ref[y * T:(y + 1) * T] = val
        rows.append(e)
    send_ref[4 * T:] = exps_block(rows)


def turn_kernel(meta, recv_ref, colt_ref, keep_ref, s1, s2, s3, tile_s):
    exps = exps_of(recv_ref[4 * T:])
    for y in range(4):
        tile_s[y] = dec(recv_ref[y * T:(y + 1) * T], exps[y:y + 1]) + colt_ref[meta[5] * 4 + y]
    keep_ref[...] = tile_s[meta[6]]
    for n, ref in enumerate((s1, s2, s3)):
        val, e = enc(tile_s[(meta[6] + n + 1) & 3])
        ref[0:T] = val
        ref[T:] = exps_block([e])


def parts_of(x):
    a = x.astype(BF16)
    rest = x - a.astype(F32)
    b = rest.astype(BF16)
    return [a, b, (rest - b.astype(F32)).astype(BF16)]


def third_kernel(meta, r2_ref, col_ref, t1, t2, t3, r_ref, dr_ref, hv_ref, out_ref, gram_s, cross_s, term_s):
    off = meta[4]
    total = col_ref[...]
    for ref in (t1, t2, t3):
        total = total + dec(ref[0:T], exps_of(ref[T:])[0:1])
    core = jnp.zeros((PIECE, T), F32)
    for z in range(NZ):
        e = exps_of(r2_ref[z, C2_EXP:])
        total = total + dec(r2_ref[z, 0:T], e[0:1])
        core = core + dec(r2_ref[z, C2_CORE:C2_GRAM], e[1:2])
        g = dec(r2_ref[z, C2_GRAM:C2_EXP], e[2:3])
        for half in range(2):
            at = (2 * z + half) * 8
            cross_s[at:at + 8] = g[half * 16:half * 16 + 8]
            gram_s[at:at + 8] = g[half * 16 + 8:half * 16 + 16]
    hv_ref[...] = (-total).astype(BF16)
    gram = gram_s[...]
    cross = cross_s[...]
    d_gram = cross + cross.T
    gram_parts, d_parts = parts_of(gram), parts_of(d_gram)
    lefts, rights = [], []
    for n in range(3):
        r, dr = r_ref[n], dr_ref[n]
        rows = jnp.concatenate([r, r, r, dr, dr, dr], axis=0)
        lefts.append(jnp.dot(jnp.concatenate(d_parts + gram_parts, axis=1), rows, preferred_element_type=F32))
        rights.append(jnp.dot(jnp.concatenate(gram_parts, axis=1), rows[:3 * T], preferred_element_type=F32))
    both = jnp.concatenate([jnp.concatenate(lefts, axis=0), jnp.concatenate(rights, axis=0)], axis=1)
    term_s[...] = jnp.dot(both, jnp.concatenate([gram, d_gram], axis=0), precision=HIGH, preferred_element_type=F32)
    val, e = enc(term_s[pl.ds(pl.multiple_of(off, 16), PIECE)] - core)
    block = exps_block([e])
    for g in range(NG):
        out_ref[g, 0:PIECE] = val
        out_ref[g, PIECE:] = block


STORES = 8


def decode(half, ref, out_hbm, buf, sems):
    copies = []
    for n in range(STORES):
        for g in range(n * NG // STORES, (n + 1) * NG // STORES):
            e = exps_of(ref[g, PIECE:])
            buf[g * PIECE:(g + 1) * PIECE] = dec(ref[g, 0:PIECE], e[0:1])
        rows = HALF // STORES
        to = pl.ds(pl.multiple_of(half * HALF + n * rows, 32), rows)
        copies.append(pltpu.make_async_copy(buf.at[pl.ds(n * rows, rows)], out_hbm.at[to], sems.at[n]))
        copies[n].start()
    for copy in copies:
        copy.wait()


def first_half(meta, ref, out_hbm, buf, sems):
    decode(meta[0], ref, out_hbm, buf, sems)


def second_half(meta, ref, before, out_hbm, buf, sems):
    decode(1 - meta[0], ref, out_hbm, buf, sems)


def shape(*dims, dtype=F32):
    return jax.ShapeDtypeStruct(dims, dtype)


VM = pl.BlockSpec(memory_space=pltpu.VMEM)
SM = pl.BlockSpec(memory_space=pltpu.SMEM)
ANY = pl.BlockSpec(memory_space=pl.ANY)
HBM = pl.BlockSpec(memory_space=pltpu.HBM)


def call(kernel, ins, outs, *args, scratch=(), flops=0, moved=0, space=None, alias=None):
    return pl.pallas_call(
        kernel, in_specs=ins, out_specs=[space or VM] * len(outs), out_shape=outs, scratch_shapes=list(scratch),
        input_output_aliases=alias or {},
        compiler_params=pltpu.CompilerParams(vmem_limit_bytes=16 * 1024 * 1024),
        cost_estimate=pl.CostEstimate(flops=flops, bytes_accessed=moved, transcendentals=0),
    )(*args)


def per_device(tile_values, tile_slots, counts, factor, d_factor, core_rel, d_core):
    held = lambda a: pltpu.with_memory_space_constraint(a, pltpu.HBM)
    swap = lambda a: lax.ppermute(a, "core", [(0, 1), (1, 0)])
    cross = lambda a: lax.ppermute(a, "xh", [(0, 1), (1, 0)])
    plane = ("xl", "xh", "y")
    exchange = lambda a, axes: lax.all_to_all(a, axes, 0, 0, tiled=True)
    c, xh, z = lax.axis_index("core"), lax.axis_index("xh"), lax.axis_index("z")
    xl, y = lax.axis_index("xl"), lax.axis_index("y")
    g = xl * 8 + xh * 4 + y
    first = c * HALF + g * PIECE
    k0 = jnp.minimum(first // T, RELS - 3)
    meta = jnp.stack([c, z * 2 + xh, xh, k0, first - k0 * T, xl, y]).astype(I32)
    slots = jnp.transpose(tile_slots[0, 0], (1, 2, 0))
    lives = jnp.arange(SC, dtype=I32)[:, None] < counts[0]
    table = jnp.concatenate([slots[:, 0], slots[:, 2], lives.astype(I32)])
    tiles = tile_values.reshape(SPANS, SC, T, T)
    r_three = lax.dynamic_slice(core_rel, (k0, 0, 0), (3, T, T))
    dr_three = lax.dynamic_slice(d_core, (k0, 0, 0), (3, T, T))

    over_xl = lambda a: lax.ppermute(a, "xl", [(0, 1), (1, 0)])
    d_there, f_there = over_xl(d_factor), over_xl(factor)
    pairs, pair = call(
        pair_kernel, [HBM] * 2, [shape(NZ, T, 2 * T, dtype=BF16), shape(T, 2 * T, dtype=BF16)],
        held(d_factor), held(factor),
        scratch=[pltpu.VMEM((T, T), BF16), pltpu.VMEM((T, T), BF16), pltpu.SemaphoreType.DMA((2,))])
    own = exchange(pairs, "z")
    two = jnp.stack([pair, jnp.concatenate([d_there, f_there], axis=1)])
    turn = lambda n: lax.ppermute(two, "y", [(i, (i + n) % 4) for i in range(4)])
    columns = (two, turn(1), turn(2), turn(3))
    own, columns, table, meta = lax.optimization_barrier((own, columns, table, meta))
    across = cross(own)
    beside = swap(own)

    near, total, *send_row = call(
        near_kernel, [SM] * 2 + [HBM] * 3 + [VM] * 4,
        [shape(SPANS, SC, T, 2 * T, dtype=BF16), shape(SPANS, T, T)]
        + [shape(ROW_EXP + 16, T, dtype=I16)] * 4,
        table, meta, held(tiles), held(core_rel), held(d_core), *columns,
        scratch=[pltpu.VMEM((SPANS, SC, T, T), BF16), pltpu.VMEM((RELS, T, T), BF16), pltpu.VMEM((RELS, T, T), BF16),
                 pltpu.VMEM((NR, T, 2 * T), BF16), pltpu.SemaphoreType.DMA((STEPS + 2,))],
        flops=6000000000, moved=16000000)
    recv_row = [swap(a) for a in send_row]
    core_a, gram_a = call(
        core_kernel_a, [SM] * 2 + [VM] * 3, [shape(RELS * T, T), shape(T, 2 * T)],
        table, meta, own, beside, near, flops=1000, moved=1000)
    keep, send_xh = call(
        row_kernel, [SM] + [VM] * 5 + [ANY],
        [shape(NZ, T, T), shape(XH_EXP + 16, T, dtype=I16)],
        meta, *recv_row, total, gram_a, flops=1000, moved=1000)
    across, sent = lax.optimization_barrier((across, send_xh))
    opposite = swap(across)
    recv_xh = cross(send_xh)
    (colt_a,) = call(
        far_kernel_a, [SM] * 2 + [VM] * 5 + [ANY], [shape(NR, T, T)],
        table, meta, own, beside, tiles, core_rel, d_core, sent, flops=3000000000, moved=1000)
    core_b, *send_core, gram = call(
        core_kernel_b, [SM] * 2 + [VM] * 5 + [ANY],
        [shape(RELS * T, T)] + [shape(CORE_EXP + 16, T, dtype=I16)] * 4 + [shape(16, T)],
        table, meta, across, opposite, near, core_a, gram_a, colt_a,
        scratch=[pltpu.VMEM((T, 2 * T), F32)], flops=1000, moved=1000)
    recv_core = [swap(a) for a in send_core]
    (colt,) = call(
        far_kernel_b, [SM] * 2 + [VM] * 6, [shape(NR, T, T)],
        table, meta, across, opposite, tiles, core_rel, d_core, colt_a, flops=1000, moved=1000)
    (c1,) = call(
        merge_kernel, [SM] + [VM] * 7 + [ANY] * 2, [shape(NG, C1_ROWS, T, dtype=I16)],
        meta, *recv_core, core_a, core_b, gram, recv_xh, colt, flops=1600000000, moved=8000000)
    r1 = exchange(c1, plane)
    c2, token = call(second_kernel, [VM] * 3, [shape(NZ, C2_ROWS, T, dtype=I16), shape(8, T)], r1, recv_xh, keep,
                 flops=1300000000, moved=4000000)
    r2 = exchange(c2, "z")
    (send_col,) = call(
        column_kernel, [SM, VM, ANY], [shape(4 * T + 16, T, dtype=I16)], meta, colt, r1, flops=600000000, moved=500000)
    col_keep, *turned = call(
        turn_kernel, [SM] + [VM] * 2, [shape(T, T)] + [shape(T + 16, T, dtype=I16)] * 3,
        meta, over_xl(send_col), colt, scratch=[pltpu.VMEM((4, T, T), F32)], flops=600000000, moved=500000)
    turned = [lax.ppermute(a, "y", [(i, (i + n + 1) % 4) for i in range(4)]) for n, a in enumerate(turned)]
    hv_factor, c3 = call(
        third_kernel, [SM] + [VM] * 7, [shape(T, T, dtype=BF16), shape(NG, C3_ROWS, T, dtype=I16)],
        meta, r2, col_keep, *turned, r_three, dr_three,
        scratch=[pltpu.VMEM((T, T), F32)] * 2 + [pltpu.VMEM((3 * T, T), F32)], flops=3000000000, moved=2000000)
    mine = exchange(c3, plane)
    other = swap(mine)

    result = shape(RELS * T, T)
    stores = [pltpu.VMEM((HALF, T), F32), pltpu.SemaphoreType.DMA((STORES,))]
    (half,) = call(first_half, [SM, VM], [result], meta, mine, scratch=stores, flops=2000000, moved=3000000, space=HBM)
    (hv_core,) = call(second_half, [SM, VM, HBM], [result], meta, other, half, scratch=stores, space=HBM, alias={2: 0})
    return hv_factor, hv_core.reshape(RELS, T, T)


def solution(mesh):
    chips = Mesh(mesh.devices.reshape(2, 4, 8, 2, 2), ("xl", "y", "z", "xh", "core"))
    row, col = ("xl", "y"), ("z", "xh", "core")
    placed = (
        P(row, col, None, None, None, None),
        P(row, col, None, None, None),
        P(row, col, None),
        P(row + col, None),
        P(row + col, None),
        P(),
        P(),
    )
    return jax.shard_map(
        per_device,
        mesh=chips,
        in_specs=placed,
        out_specs=(P(row + col, None), P()),
        check_vma=False,
    )
```

```python
import jax
import jax.numpy as jnp
from jax import lax
from jax.experimental import pallas as pl
from jax.experimental.pallas import tpu as pltpu
from jax.sharding import Mesh
from jax.sharding import PartitionSpec as P

F32 = jnp.float32
BF16 = jnp.bfloat16
I16 = jnp.int16
I32 = jnp.int32
HIGH = lax.Precision.HIGHEST

T = 128
SC = 3
SPANS = 32
NR = 8
NZ = 8
UNROLL = 8
STEPS = SPANS // UNROLL
NG = 16
NQ = 16
RELS = 60
HALF = RELS // 2 * T
PIECE = HALF // NG
ROW_EXP = 4 * T
CORE_EXP = 4 * PIECE
XH_EXP = NZ * T
C1_GRAM = PIECE
C1_EXP = C1_GRAM + 16
C1_ROWS = C1_EXP + 16
C2_CORE = T
C2_GRAM = C2_CORE + PIECE
C2_EXP = C2_GRAM + 32
C2_ROWS = C2_EXP + 16
C3_ROWS = PIECE + 16

NT = (((1,), (1,)), ((), ()))
TN = (((0,), (0,)), ((), ()))


def exponent_of(x):
    top = jnp.max(jnp.abs(x), axis=0, keepdims=True)
    e = jnp.floor(jnp.log2(jnp.maximum(top, 1e-37))) + 1.0
    return jnp.clip(e, -100.0, 127.0)


def coded(x, e):
    q = jnp.round(x * jnp.exp2(15.0 - e))
    return jnp.clip(q, -32767.0, 32767.0).astype(I32)


def enc(x):
    e = exponent_of(x)
    return coded(x, e).astype(I16), e


def dec(q, e):
    return q.astype(I32).astype(F32) * jnp.exp2(e - 15.0)


def exps_of(block):
    return block.astype(I32).astype(F32)


def exps_block(rows):
    place = lax.broadcasted_iota(I32, (16, T), 0)
    out = jnp.zeros((16, T), F32)
    for r, e in enumerate(rows):
        out = jnp.where(place == r, e, out)
    return out.astype(I32).astype(I16)


def pair_kernel(d_hbm, f_hbm, wide_ref, one_ref, d_s, f_s, sems):
    one = pltpu.make_async_copy(d_hbm, d_s, sems.at[0])
    two = pltpu.make_async_copy(f_hbm, f_s, sems.at[1])
    one.start()
    two.start()
    one.wait()
    two.wait()
    one_ref[:, 0:T] = d_s[...]
    one_ref[:, T:] = f_s[...]
    for i in range(NZ):
        wide_ref[i] = one_ref[...]


def near_kernel(table, meta, x_hbm, r_hbm, dr_hbm, c0, c1, c2, c3,
                near_ref, total_ref, s0, s1, s2, s3, x_s, r_s, dr_s, col_s, sems):
    tiles = [pltpu.make_async_copy(x_hbm.at[pl.ds(n * UNROLL, UNROLL)], x_s.at[pl.ds(n * UNROLL, UNROLL)], sems.at[n])
             for n in range(STEPS)]
    cores = [pltpu.make_async_copy(r_hbm, r_s, sems.at[STEPS]), pltpu.make_async_copy(dr_hbm, dr_s, sems.at[STEPS + 1])]
    for copy in tiles + cores:
        copy.start()
    for n, ref in enumerate((c0, c1, c2, c3)):
        col_s[2 * n] = ref[0]
        col_s[2 * n + 1] = ref[1]
    xl, y = meta[5], meta[6]

    for step in range(STEPS):
        tiles[step].wait()
        for j in range(UNROLL):
            span = step * UNROLL + j
            for s in range(SC):
                b = table[3 + s, span]
                at = ((y - b) & 3) * 2 + ((b >> 2) ^ xl)
                x = x_s[span, s]
                if s > 0:
                    x = jnp.where(table[6 + s, span] > 0, x, jnp.zeros_like(x))
                near_ref[span, s] = jnp.dot(x, col_s[at], preferred_element_type=F32).astype(BF16)
    for copy in cores:
        copy.wait()

    for span in range(SPANS):
        total = None
        for s in range(SC):
            k = table[s, span]
            both = jnp.concatenate([r_s[k], dr_s[k]], axis=1)
            term = lax.dot_general(near_ref[span, s], both, NT, preferred_element_type=F32)
            total = term if total is None else total + term
        total_ref[span] = total

    for n, send_ref in enumerate((s0, s1, s2, s3)):
        rows = []
        for q in range(4):
            val, e = enc(total_ref[(n * 4 + q) * 2 + 1 - meta[0]])
            send_ref[q * T:(q + 1) * T] = val
            rows.append(e)
        send_ref[ROW_EXP:] = exps_block(rows)


def spans_of(meta, z, far_chip):
    c = meta[0]
    xh = 1 - meta[2] if far_chip else meta[2]
    return z * 4 + xh * 2 + c, z * 4 + xh * 2 + 1 - c


def core_sums(far_chip, table, meta, refs, near_ref, core_ref, gram_ref):
    core_ref[...] = jnp.zeros_like(core_ref)
    gram = jnp.zeros((T, 2 * T), F32)
    for z in range(NZ):
        for span, ref in zip(spans_of(meta, z, far_chip), refs):
            rows = ref[z]
            rows_t = rows.T
            gram = gram + jnp.dot(rows_t[T:], rows, preferred_element_type=F32)
            lhs = jnp.concatenate([rows_t[T:], rows_t[:T]], axis=1)
            near = [near_ref[span, s] for s in range(SC)]
            near = jnp.concatenate([jnp.concatenate([n[:, :T] for n in near], axis=1),
                                    jnp.concatenate([n[:, T:] for n in near], axis=1)], axis=0)
            terms = jnp.dot(lhs, near, preferred_element_type=F32)
            for s in range(SC):
                place = pl.ds(pl.multiple_of(table[s, span] * T, T), T)
                core_ref[place] += terms[:, s * T:(s + 1) * T]
    gram_ref[...] = gram


def core_kernel_a(table, meta, r0, r1, near_ref, core_ref, gram_ref):
    core_sums(False, table, meta, (r0, r1), near_ref, core_ref, gram_ref)


def core_kernel_b(table, meta, r0, r1, near_ref, held_ref, gram_held, after, core_ref, s0, s1, s2, s3, gram_out, gram_acc):
    core_sums(True, table, meta, (r0, r1), near_ref, core_ref, gram_acc)
    start = (1 - meta[0]) * HALF
    for n, send_ref in enumerate((s0, s1, s2, s3)):
        rows = []
        for g in range(4):
            at = pl.ds(pl.multiple_of(start + (n * 4 + g) * PIECE, 16), PIECE)
            val, e = enc(core_ref[at] + held_ref[at])
            send_ref[g * PIECE:(g + 1) * PIECE] = val
            rows.append(e)
        send_ref[CORE_EXP:] = exps_block(rows)
    at = pl.ds(pl.multiple_of(meta[1] * 8, 8), 8)
    part = gram_acc[at] + gram_held[at]
    gram_out[0:8] = part[:, :T]
    gram_out[8:16] = part[:, T:]


def far_sums(far_chip, table, meta, refs, x_ref, r_ref, dr_ref, colt_ref):
    for z in range(NZ):
        for span, ref in zip(spans_of(meta, z, far_chip), refs):
            x = [x_ref[span, s] for s in range(SC)]
            x[1:] = [jnp.where(table[6 + s, span] > 0, x[s], jnp.zeros_like(x[s])) for s in range(1, SC)]
            far = lax.dot_general(jnp.concatenate(x, axis=1), ref[z], TN, preferred_element_type=F32).astype(BF16)
            for s in range(SC):
                k = table[s, span]
                colt_ref[table[3 + s, span]] += jnp.dot(
                    far[s * T:(s + 1) * T], jnp.concatenate([r_ref[k], dr_ref[k]], axis=0), preferred_element_type=F32)


def far_kernel_a(table, meta, r0, r1, x_ref, r_ref, dr_ref, after, colt_ref):
    colt_ref[...] = jnp.zeros_like(colt_ref)
    far_sums(False, table, meta, (r0, r1), x_ref, r_ref, dr_ref, colt_ref)


def far_kernel_b(table, meta, r0, r1, x_ref, r_ref, dr_ref, held_ref, colt_ref):
    colt_ref[...] = held_ref[...]
    far_sums(True, table, meta, (r0, r1), x_ref, r_ref, dr_ref, colt_ref)


def row_kernel(meta, v0, v1, v2, v3, total_ref, after, keep_ref, send_ref):
    c, xh = meta[0], meta[2]
    recv = (v0, v1, v2, v3)
    exps = [exps_of(ref[ROW_EXP:]) for ref in recv]
    merged = []
    for q in range(NQ):
        n, at = q // 4, q % 4
        merged.append(dec(recv[n][at * T:(at + 1) * T], exps[n][at:at + 1]) + total_ref[q * 2 + c])
    rows = []
    for z in range(NZ):
        a, b = merged[2 * z], merged[2 * z + 1]
        keep_ref[z] = jnp.where(xh == 0, a, b)
        val, e = enc(jnp.where(xh == 0, b, a))
        send_ref[z * T:(z + 1) * T] = val
        rows.append(e)
    send_ref[XH_EXP:] = exps_block(rows)


def merge_kernel(meta, v0, v1, v2, v3, core_a, core_b, gram_ref, after, done, out_ref):
    recv = (v0, v1, v2, v3)
    exps = [exps_of(ref[CORE_EXP:]) for ref in recv]
    gram, g_e = enc(gram_ref[...])
    start = meta[0] * HALF
    for g in range(NG):
        n, at = g // 4, g % 4
        got = dec(recv[n][at * PIECE:(at + 1) * PIECE], exps[n][at:at + 1])
        at = pl.ds(pl.multiple_of(start + g * PIECE, 16), PIECE)
        val, e = enc(got + core_a[at] + core_b[at])
        out_ref[g, 0:C1_GRAM] = val
        out_ref[g, C1_GRAM:C1_EXP] = gram
        out_ref[g, C1_EXP:] = exps_block([e, g_e])


def second_kernel(r1_ref, recv_ref, keep_ref, out_ref, token_ref):
    gram = [jnp.zeros((16, T), F32) for _ in range(2)]
    core = jnp.zeros((PIECE, T), F32)
    for g in range(NG):
        xh = g // 4 % 2
        e = exps_of(r1_ref[g, C1_EXP:])
        core = core + dec(r1_ref[g, 0:C1_GRAM], e[0:1])
        gram[xh] = gram[xh] + dec(r1_ref[g, C1_GRAM:C1_EXP], e[1:2])
    core, e1 = enc(core)
    gram, g_e = enc(jnp.concatenate(gram, axis=0))
    exps = exps_of(recv_ref[XH_EXP:])
    token_ref[...] = jnp.zeros_like(token_ref)
    for z in range(NZ):
        val, e0 = enc(dec(recv_ref[z * T:(z + 1) * T], exps[z:z + 1]) + keep_ref[z])
        out_ref[z, 0:C2_CORE] = val
        out_ref[z, C2_CORE:C2_GRAM] = core
        out_ref[z, C2_GRAM:C2_EXP] = gram
        out_ref[z, C2_EXP:] = exps_block([e0, e1, g_e])


def column_kernel(meta, colt_ref, after, send_ref):
    rows = []
    for y in range(4):
        val, e = enc(colt_ref[(1 - meta[5]) * 4 + y])
        send_ref[y * T:(y + 1) * T] = val
        rows.append(e)
    send_ref[4 * T:] = exps_block(rows)


def turn_kernel(meta, recv_ref, colt_ref, keep_ref, s1, s2, s3, tile_s):
    exps = exps_of(recv_ref[4 * T:])
    for y in range(4):
        tile_s[y] = dec(recv_ref[y * T:(y + 1) * T], exps[y:y + 1]) + colt_ref[meta[5] * 4 + y]
    keep_ref[...] = tile_s[meta[6]]
    for n, ref in enumerate((s1, s2, s3)):
        val, e = enc(tile_s[(meta[6] + n + 1) & 3])
        ref[0:T] = val
        ref[T:] = exps_block([e])


def parts_of(x):
    a = x.astype(BF16)
    rest = x - a.astype(F32)
    b = rest.astype(BF16)
    return [a, b, (rest - b.astype(F32)).astype(BF16)]


def third_kernel(meta, r2_ref, col_ref, t1, t2, t3, r_ref, dr_ref, hv_ref, out_ref, gram_s, cross_s, term_s):
    off = meta[4]
    total = col_ref[...]
    for ref in (t1, t2, t3):
        total = total + dec(ref[0:T], exps_of(ref[T:])[0:1])
    core = jnp.zeros((PIECE, T), F32)
    for z in range(NZ):
        e = exps_of(r2_ref[z, C2_EXP:])
        total = total + dec(r2_ref[z, 0:T], e[0:1])
        core = core + dec(r2_ref[z, C2_CORE:C2_GRAM], e[1:2])
        g = dec(r2_ref[z, C2_GRAM:C2_EXP], e[2:3])
        for half in range(2):
            at = (2 * z + half) * 8
            cross_s[at:at + 8] = g[half * 16:half * 16 + 8]
            gram_s[at:at + 8] = g[half * 16 + 8:half * 16 + 16]
    hv_ref[...] = (-total).astype(BF16)
    gram = gram_s[...]
    cross = cross_s[...]
    d_gram = cross + cross.T
    gram_parts, d_parts = parts_of(gram), parts_of(d_gram)
    lefts, rights = [], []
    for n in range(3):
        r, dr = r_ref[n], dr_ref[n]
        rows = jnp.concatenate([r, r, r, dr, dr, dr], axis=0)
        lefts.append(jnp.dot(jnp.concatenate(d_parts + gram_parts, axis=1), rows, preferred_element_type=F32))
        rights.append(jnp.dot(jnp.concatenate(gram_parts, axis=1), rows[:3 * T], preferred_element_type=F32))
    both = jnp.concatenate([jnp.concatenate(lefts, axis=0), jnp.concatenate(rights, axis=0)], axis=1)
    term_s[...] = jnp.dot(both, jnp.concatenate([gram, d_gram], axis=0), precision=HIGH, preferred_element_type=F32)
    val, e = enc(term_s[pl.ds(pl.multiple_of(off, 16), PIECE)] - core)
    block = exps_block([e])
    for g in range(NG):
        out_ref[g, 0:PIECE] = val
        out_ref[g, PIECE:] = block


STORES = 8


def decode(half, ref, out_hbm, buf, sems):
    copies = []
    for n in range(STORES):
        for g in range(n * NG // STORES, (n + 1) * NG // STORES):
            e = exps_of(ref[g, PIECE:])
            buf[g * PIECE:(g + 1) * PIECE] = dec(ref[g, 0:PIECE], e[0:1])
        rows = HALF // STORES
        to = pl.ds(pl.multiple_of(half * HALF + n * rows, 32), rows)
        copies.append(pltpu.make_async_copy(buf.at[pl.ds(n * rows, rows)], out_hbm.at[to], sems.at[n]))
        copies[n].start()
    for copy in copies:
        copy.wait()


def first_half(meta, ref, out_hbm, buf, sems):
    decode(meta[0], ref, out_hbm, buf, sems)


def second_half(meta, ref, before, out_hbm, buf, sems):
    decode(1 - meta[0], ref, out_hbm, buf, sems)


def shape(*dims, dtype=F32):
    return jax.ShapeDtypeStruct(dims, dtype)


VM = pl.BlockSpec(memory_space=pltpu.VMEM)
SM = pl.BlockSpec(memory_space=pltpu.SMEM)
ANY = pl.BlockSpec(memory_space=pl.ANY)
HBM = pl.BlockSpec(memory_space=pltpu.HBM)


def call(kernel, ins, outs, *args, scratch=(), flops=0, moved=0, space=None, alias=None):
    return pl.pallas_call(
        kernel, in_specs=ins, out_specs=[space or VM] * len(outs), out_shape=outs, scratch_shapes=list(scratch),
        input_output_aliases=alias or {},
        compiler_params=pltpu.CompilerParams(vmem_limit_bytes=16 * 1024 * 1024),
        cost_estimate=pl.CostEstimate(flops=flops, bytes_accessed=moved, transcendentals=0),
    )(*args)


def per_device(tile_values, tile_slots, counts, factor, d_factor, core_rel, d_core):
    held = lambda a: pltpu.with_memory_space_constraint(a, pltpu.HBM)
    swap = lambda a: lax.ppermute(a, "core", [(0, 1), (1, 0)])
    cross = lambda a: lax.ppermute(a, "xh", [(0, 1), (1, 0)])
    plane = ("xl", "xh", "y")
    exchange = lambda a, axes: lax.all_to_all(a, axes, 0, 0, tiled=True)
    c, xh, z = lax.axis_index("core"), lax.axis_index("xh"), lax.axis_index("z")
    xl, y = lax.axis_index("xl"), lax.axis_index("y")
    g = xl * 8 + xh * 4 + y
    first = c * HALF + g * PIECE
    k0 = jnp.minimum(first // T, RELS - 3)
    meta = jnp.stack([c, z * 2 + xh, xh, k0, first - k0 * T, xl, y]).astype(I32)
    slots = jnp.transpose(tile_slots[0, 0], (1, 2, 0))
    lives = jnp.arange(SC, dtype=I32)[:, None] < counts[0]
    table = jnp.concatenate([slots[:, 0], slots[:, 2], lives.astype(I32)])
    tiles = tile_values.reshape(SPANS, SC, T, T)
    r_three = lax.dynamic_slice(core_rel, (k0, 0, 0), (3, T, T))
    dr_three = lax.dynamic_slice(d_core, (k0, 0, 0), (3, T, T))

    over_xl = lambda a: lax.ppermute(a, "xl", [(0, 1), (1, 0)])
    d_there, f_there = over_xl(d_factor), over_xl(factor)
    pairs, pair = call(
        pair_kernel, [HBM] * 2, [shape(NZ, T, 2 * T, dtype=BF16), shape(T, 2 * T, dtype=BF16)],
        held(d_factor), held(factor),
        scratch=[pltpu.VMEM((T, T), BF16), pltpu.VMEM((T, T), BF16), pltpu.SemaphoreType.DMA((2,))])
    own = exchange(pairs, "z")
    two = jnp.stack([pair, jnp.concatenate([d_there, f_there], axis=1)])
    turn = lambda n: lax.ppermute(two, "y", [(i, (i + n) % 4) for i in range(4)])
    columns = (two, turn(1), turn(2), turn(3))
    own, columns, table, meta = lax.optimization_barrier((own, columns, table, meta))
    across = cross(own)
    beside = swap(own)

    near, total, *send_row = call(
        near_kernel, [SM] * 2 + [HBM] * 3 + [VM] * 4,
        [shape(SPANS, SC, T, 2 * T, dtype=BF16), shape(SPANS, T, T)]
        + [shape(ROW_EXP + 16, T, dtype=I16)] * 4,
        table, meta, held(tiles), held(core_rel), held(d_core), *columns,
        scratch=[pltpu.VMEM((SPANS, SC, T, T), BF16), pltpu.VMEM((RELS, T, T), BF16), pltpu.VMEM((RELS, T, T), BF16),
                 pltpu.VMEM((NR, T, 2 * T), BF16), pltpu.SemaphoreType.DMA((STEPS + 2,))],
        flops=6000000000, moved=16000000)
    recv_row = [swap(a) for a in send_row]
    core_a, gram_a = call(
        core_kernel_a, [SM] * 2 + [VM] * 3, [shape(RELS * T, T), shape(T, 2 * T)],
        table, meta, own, beside, near, flops=1000, moved=1000)
    keep, send_xh = call(
        row_kernel, [SM] + [VM] * 5 + [ANY],
        [shape(NZ, T, T), shape(XH_EXP + 16, T, dtype=I16)],
        meta, *recv_row, total, gram_a, flops=1000, moved=1000)
    across, sent = lax.optimization_barrier((across, send_xh))
    opposite = swap(across)
    recv_xh = cross(send_xh)
    (colt_a,) = call(
        far_kernel_a, [SM] * 2 + [VM] * 5 + [ANY], [shape(NR, T, T)],
        table, meta, own, beside, tiles, core_rel, d_core, sent, flops=3000000000, moved=1000)
    core_b, *send_core, gram = call(
        core_kernel_b, [SM] * 2 + [VM] * 5 + [ANY],
        [shape(RELS * T, T)] + [shape(CORE_EXP + 16, T, dtype=I16)] * 4 + [shape(16, T)],
        table, meta, across, opposite, near, core_a, gram_a, colt_a,
        scratch=[pltpu.VMEM((T, 2 * T), F32)], flops=1000, moved=1000)
    recv_core = [swap(a) for a in send_core]
    (colt,) = call(
        far_kernel_b, [SM] * 2 + [VM] * 6, [shape(NR, T, T)],
        table, meta, across, opposite, tiles, core_rel, d_core, colt_a, flops=1000, moved=1000)
    (c1,) = call(
        merge_kernel, [SM] + [VM] * 7 + [ANY] * 2, [shape(NG, C1_ROWS, T, dtype=I16)],
        meta, *recv_core, core_a, core_b, gram, recv_xh, colt, flops=1600000000, moved=8000000)
    r1 = exchange(c1, plane)
    c2, token = call(second_kernel, [VM] * 3, [shape(NZ, C2_ROWS, T, dtype=I16), shape(8, T)], r1, recv_xh, keep,
                 flops=1300000000, moved=4000000)
    r2 = exchange(c2, "z")
    (send_col,) = call(
        column_kernel, [SM, VM, ANY], [shape(4 * T + 16, T, dtype=I16)], meta, colt, r1, flops=600000000, moved=500000)
    col_keep, *turned = call(
        turn_kernel, [SM] + [VM] * 2, [shape(T, T)] + [shape(T + 16, T, dtype=I16)] * 3,
        meta, over_xl(send_col), colt, scratch=[pltpu.VMEM((4, T, T), F32)], flops=600000000, moved=500000)
    turned = [lax.ppermute(a, "y", [(i, (i + n + 1) % 4) for i in range(4)]) for n, a in enumerate(turned)]
    hv_factor, c3 = call(
        third_kernel, [SM] + [VM] * 7, [shape(T, T, dtype=BF16), shape(NG, C3_ROWS, T, dtype=I16)],
        meta, r2, col_keep, *turned, r_three, dr_three,
        scratch=[pltpu.VMEM((T, T), F32)] * 2 + [pltpu.VMEM((3 * T, T), F32)], flops=3000000000, moved=2000000)
    mine = exchange(c3, plane)
    other = swap(mine)

    result = shape(RELS * T, T)
    stores = [pltpu.VMEM((HALF, T), F32), pltpu.SemaphoreType.DMA((STORES,))]
    (half,) = call(first_half, [SM, VM], [result], meta, mine, scratch=stores, flops=2000000, moved=3000000, space=HBM)
    (hv_core,) = call(second_half, [SM, VM, HBM], [result], meta, other, half, scratch=stores, space=HBM, alias={2: 0})
    return hv_factor, hv_core.reshape(RELS, T, T)


def solution(mesh):
    chips = Mesh(mesh.devices.reshape(2, 4, 8, 2, 2), ("xl", "y", "z", "xh", "core"))
    row, col = ("xl", "y"), ("z", "xh", "core")
    placed = (
        P(row, col, None, None, None, None),
        P(row, col, None, None, None),
        P(row, col, None),
        P(row + col, None),
        P(row + col, None),
        P(),
        P(),
    )
    return jax.shard_map(
        per_device,
        mesh=chips,
        in_specs=placed,
        out_specs=(P(row + col, None), P()),
        check_vma=False,
    )
```
